512 devices in a mesh: blk: 64 (over z_hi, x, y), rd: 8 (over z_lo, core).
Axes of the slice: x: 4, y: 8, z: 8 (z_hi: 2, z_lo: 4; z = z_hi * 4 + z_lo), core: 2. Of those that a mesh axis runs over, the one named last changes fastest.
Arguments:
- factor: float32 [18432, 8, 2304], P('blk', 'rd'), as said below
- panel: float32 [18432, 1024], P(('blk', 'rd')), may hold values from -6 to 6
Outputs:
- new_panel: float32 [18432, 1024], P('blk')
- values: float32 [1024], replicated
The draws below stay inside these ranges and needn't reach their ends.
Inputs may be any that keep to these rules, and one draw needn't show every extreme that they name: L built from factor is symmetric and positive definite.
All inputs are finite; a program needn't handle non-finite values.
Results may differ from the reference program's by a relative error of at most 0.000073.
Values sent between devices are 32-bit elements; how exact they have to be, the bound alone decides.
A program may use at most 128 MiB of HBM per device.

```python
import jax
import jax.numpy as jnp
from jax import lax

N = 18432
P_SIZE = 1024
N_BLK = 64
N_RD = 8


def draw_factor(key, part):
    key = jax.random.fold_in(key, 1)
    first, second, third = jax.random.split(key, 3)
    noise = jnp.clip(jax.random.normal(first, (N, N), jnp.float32), -6.0, 6.0)
    rise = 2.0
    symmetric = (noise + noise.T) * (0.5 / jnp.sqrt(2.0 * N))
    diag_part = 3.0 + jax.random.uniform(second, (N,), jnp.float32)
    index = jnp.arange(N)
    middle = jnp.where(index[:, None] == index[None, :], diag_part[None, :], symmetric)
    ramp = 1.0 + rise * index.astype(jnp.float32) / (N - 1)
    spread = jnp.exp(jax.random.uniform(third, (N,), jnp.float32, jnp.log(0.7), jnp.log(1.4)))
    scales = ramp * spread
    matrix = scales[:, None] * middle * scales[None, :]
    blocks = matrix.reshape(N, N_BLK, N_RD, N // (N_BLK * N_RD))
    return jnp.transpose(blocks, (0, 2, 1, 3)).reshape(N, N_RD, N // N_RD)


def steps_of(stream_key, dims, cuts, low, high):
    loudness = 1.0
    for axis_at, shards_of in cuts:
        draws = jax.random.uniform(jax.random.fold_in(jax.random.fold_in(stream_key, 6), axis_at), (shards_of,), jnp.float32, low / len(cuts), high / len(cuts))
        loudness = loudness * jnp.repeat(jnp.exp(draws), dims[axis_at] // shards_of).reshape((-1,) + (1,) * (len(dims) - 1 - axis_at))
    return loudness


def centred(stream_key, shape, deviation, reach, shards=(), held_as=jnp.bfloat16):
    drawn = deviation * jax.random.normal(stream_key, shape, jnp.float32)
    if shards:
        drawn = drawn * steps_of(stream_key, shape, shards, -0.22, 0.18)
    return jnp.clip(drawn, -reach, reach).astype(held_as)


def setup_inputs(seed: int = 0) -> dict:
    arg_keys = jax.random.split(jax.random.key(seed), 3)
    factor = draw_factor(jax.random.fold_in(arg_keys[2], 71), 0)
    panel = centred(arg_keys[1], (N, P_SIZE), 1.0, 6.0, ((0, 512),), jnp.float32)
    return dict(factor=factor, panel=panel)


def full_factor(factor):
    blocks = factor.reshape(N, N_RD, N_BLK, N // (N_BLK * N_RD))
    return jnp.transpose(blocks, (0, 2, 1, 3)).reshape(N, N)

def reference(factor, panel):
    matrix = full_factor(factor)
    image = jnp.dot(matrix.astype(jnp.float32), panel.astype(jnp.float32), precision=lax.Precision.HIGHEST, preferred_element_type=jnp.float32)
    gram = jnp.dot(image.T.astype(jnp.float32), image.astype(jnp.float32), precision=lax.Precision.HIGHEST, preferred_element_type=jnp.float32) / N
    lower = jnp.linalg.cholesky(gram)
    new_panel = jax.scipy.linalg.solve_triangular(lower, image.T, lower=True).T
    numer = jnp.sum(panel * image, axis=0) / N
    denom = jnp.sum(panel * panel, axis=0) / N + 1e-06
    values = numer / denom
    return (new_panel, values)
```

```python
import heapq

import jax
import jax.numpy as jnp
from jax import lax
from jax.experimental import pallas as pl
from jax.experimental.pallas import tpu as pltpu
from jax.sharding import PartitionSpec as P

N = 18432
X, Y, Z = 4, 8, 4
ROWS = 36
SHARD = ROWS * 8
BLOCK = 288
CHUNK = 80
SLICE = 8 * CHUNK
MESH = pl.DeviceIdType.MESH
HIGHEST = lax.Precision.HIGHEST


def nt(a, b):
    return lax.dot_general(
        a,
        b,
        (((1,), (1,)), ((), ())),
        precision=HIGHEST,
        preferred_element_type=jnp.float32,
    )


def ring(n):
    h = n // 2
    for sign in (1, -1):
        for t in range(h - 1):
            yield sign, sign * t, None
        yield sign, sign * (h - 1), 0 if sign > 0 else 1


def order(messages, preset=()):
    waiting = {k: set(m[3]) - set(preset) for k, m in messages.items()}
    followers = {}
    for k, m in messages.items():
        for d in m[3]:
            followers.setdefault(d, []).append(k)
    free, heap, events = {}, [], []

    def start(k, now):
        link, size, latency, _ = messages[k]
        begin = max(now, free.get(link, 0.0))
        free[link] = begin + size
        events.append(("start", k))
        heapq.heappush(heap, (begin + size + latency, len(events), k))

    for k in messages:
        if not waiting[k]:
            start(k, 0.0)
    while heap:
        now, _, k = heapq.heappop(heap)
        events.append(("wait", k))
        for f in followers.get(k, ()):
            waiting[f].discard(k)
            if not waiting[f]:
                start(f, now)
    assert sum(e == "start" for e, _ in events) == len(messages)
    return events


def panel_messages():
    rate = 50e3
    out = {}
    meta = {}
    z_key = ("z",)
    out[z_key] = ("z", SHARD * 512 / 25e3, 3.0, ())
    meta[z_key] = ("z", 0, 0, 0, 0, SHARD)
    for z in range(2):
        base = (z_key,) if z else ()
        for part, (first, rows) in enumerate(((0, 22), (22, 14))):
            axes = (("y", Y), ("x", X)) if part == 0 else (("x", X), ("y", Y))
            (f_name, f_n), (s_name, s_n) = axes
            half = rows // 2

            def cut(piece):
                return (first, rows) if piece is None else (first + piece * half, half)

            def offset(f, s):
                return (f, s) if f_name == "x" else (s, f)

            delivered = {0: base}
            for sign, at, piece in ring(f_n):
                key = (z, part, "f", 0, sign, at)
                dep = base if at == 0 else ((z, part, "f", 0, sign, at - sign),)
                start, count = cut(piece)
                ox, oy = offset(at, 0)
                out[key] = (f_name + str(sign), count * 4096 / rate, 1.0, dep)
                meta[key] = (f_name, sign, z, ox, oy, start * 8, count * 8)
                to = (at + sign) % f_n
                delivered[to] = delivered.get(to, ()) + (key,)
            for f in sorted(delivered, key=lambda v: min(v, f_n - v)):
                for sign, at, piece in ring(s_n):
                    key = (z, part, "s", f, sign, at)
                    dep = delivered[f] if at == 0 else ((z, part, "s", f, sign, at - sign),)
                    start, count = cut(piece)
                    ox, oy = offset(f, at)
                    out[key] = (s_name + str(sign), count * 4096 / rate, 1.0, dep)
                    meta[key] = (s_name, sign, z, ox, oy, start * 8, count * 8)
    return out, meta


def gram_messages():
    out = {}
    meta = {}
    delivered = {0: ()}
    for sign, at, piece in ring(Y):
        key = ("y", sign, at)
        dep = () if at == 0 else (("y", sign, at - sign),)
        first, count = (0, Z) if piece is None else (piece * Z // 2, Z // 2)
        out[key] = ("y" + str(sign), count * CHUNK * 512 / 50e3, 1.0, dep)
        meta[key] = ("y", sign, at, first, count)
        to = (at + sign) % Y
        delivered[to] = delivered.get(to, ()) + (key,)
    for f, dep in delivered.items():
        key = ("core", f)
        out[key] = ("core", Z * CHUNK * 512 / 400e3, 0.5, dep)
        meta[key] = ("core", 0, f, 0, Z)
    return out, meta


PANEL_MESSAGES, PANEL_META = panel_messages()
PANEL_EVENTS = order(PANEL_MESSAGES)
PANEL_SLOT = {k: i for i, k in enumerate(PANEL_MESSAGES)}
GRAM_MESSAGES, GRAM_META = gram_messages()
GRAM_EVENTS = order(GRAM_MESSAGES)
GRAM_SLOT = {k: i for i, k in enumerate(GRAM_MESSAGES)}


def combine_kernel(
    factor_ref,
    panel_ref,
    image_ref,
    parts_ref,
    gathered,
    high,
    low,
    partial,
    from_core,
    from_z,
    local,
    from_y,
    total_y,
    from_x,
    total_x,
    from_hi,
    p_send,
    p_recv,
    r_send,
    r_recv,
    a_send,
    a_recv,
    y_send,
    y_recv,
    x_send,
    x_recv,
    h_send,
    h_recv,
    c_send,
    c_recv,
    g_send,
    g_recv,
):
    blk = lax.axis_index("blk")
    rd = lax.axis_index("rd")
    hi, x, y = blk // (X * Y), (blk // Y) % X, blk % Y
    z, core = rd // 2, rd % 2

    def at_blk(h, i, j):
        return (h * X + i) * Y + j

    def wrap(v, n):
        return lax.rem(v + n, n)

    def x_peer(d):
        return (at_blk(hi, wrap(x + d, X), y), rd)

    def y_peer(d):
        return (at_blk(hi, x, wrap(y + d, Y)), rd)

    def z_peer(d):
        return (blk, wrap(z + d, Z) * 2 + core)

    hi_peer = (at_blk(1 - hi, x, y), rd)
    core_peer = (blk, z * 2 + 1 - core)

    def remote(src, dst, send, recv, peer):
        return pltpu.make_async_remote_copy(
            src_ref=src,
            dst_ref=dst,
            send_sem=send,
            recv_sem=recv,
            device_id=peer,
            device_id_type=MESH,
        )

    barrier = pltpu.get_barrier_semaphore()
    peers = [x_peer(d) for d in range(1, X)] + [y_peer(d) for d in range(1, Y)]
    peers += [z_peer(d) for d in range(1, Z)] + [hi_peer, core_peer]
    for peer in peers:
        pl.semaphore_signal(barrier, inc=1, device_id=peer, device_id_type=MESH)

    own = pl.multiple_of(blk * SHARD, 8)
    gathered[pl.ds(own, SHARD), :] = panel_ref[...]
    pl.semaphore_wait(barrier, len(peers))

    def panel_copy(key, arrived):
        axis, sign, far, ox, oy, *span = PANEL_META[key]
        slot = PANEL_SLOT[key]
        if axis == "z":
            peer = hi_peer
            source = 1 - hi if arrived else hi
            start, count = 0, SHARD
            origin = at_blk(source, x, y)
        else:
            peer = x_peer(sign) if axis == "x" else y_peer(sign)
            start, count = span
            if arrived:
                ox, oy = (ox + sign, oy) if axis == "x" else (ox, oy + sign)
            source = 1 - hi if far else hi
            origin = at_blk(source, wrap(x - ox % X, X), wrap(y - oy % Y, Y))
        where = pl.ds(pl.multiple_of(origin * SHARD + start, 8), count)
        return remote(
            gathered.at[where], gathered.at[where], p_send.at[slot], p_recv.at[slot], peer
        )

    started = 0
    for event, key in PANEL_EVENTS:
        if event == "start":
            panel_copy(key, False).start()
        else:
            if started == 0:
                started = 1

                def split(i, carry):
                    rows = pl.ds(pl.multiple_of(i * 16, 16), 16)
                    value = factor_ref[rows, :]
                    top = value.astype(jnp.bfloat16)
                    high[rows, :] = top
                    low[rows, :] = (value - top.astype(jnp.float32)).astype(jnp.bfloat16)
                    return carry

                lax.fori_loop(0, BLOCK // 16, split, 0)
            panel_copy(key, True).wait_recv()
    for key in PANEL_MESSAGES:
        panel_copy(key, False).wait_send()

    for q in range(4):
        right = jnp.concatenate(
            [gathered[pl.ds(2 * q + s, 8 * BLOCK, stride=8), :] for s in range(2)], axis=1
        )
        r_top = right.astype(jnp.bfloat16)
        r_low = (right - r_top.astype(jnp.float32)).astype(jnp.bfloat16)
        product = (
            jnp.dot(low[...], r_top, preferred_element_type=jnp.float32)
            + jnp.dot(high[...], r_low, preferred_element_type=jnp.float32)
            + jnp.dot(high[...], r_top, preferred_element_type=jnp.float32)
        )
        partial[q, 0] = product[:, :128]
        partial[q, 1] = product[:, 128:]

    to_core = remote(
        partial.at[:, 1 - core], from_core, r_send.at[0], r_recv.at[0], core_peer
    )
    to_core.start()
    to_core.wait()
    for k in range(Z):
        from_core[k] += partial[k, core]
    to_z = [
        remote(
            from_core.at[wrap(z + d, Z)],
            from_z.at[d - 1],
            r_send.at[d],
            r_recv.at[d],
            z_peer(d),
        )
        for d in range(1, Z)
    ]
    for copy in to_z:
        copy.start()
    for copy in to_z:
        copy.wait()
    image_ref[z, core] = from_core[z] + from_z[0] + from_z[1] + from_z[2]

    def spread(d, arrived):
        who = wrap(z - d, Z) if arrived else z
        where = image_ref.at[who, core]
        return remote(where, where, a_send.at[d], a_recv.at[d], z_peer(d))

    def share(k, arrived):
        who = wrap(z - k, Z)
        where = image_ref.at[who, 1 - core if arrived else core]
        return remote(where, where, a_send.at[Z + k], a_recv.at[Z + k], core_peer)

    for d in range(1, Z):
        spread(d, False).start()
    share(0, False).start()
    for d in range(1, Z):
        spread(d, True).wait_recv()
        share(d, False).start()
    for d in range(Z):
        share(d, True).wait_recv()
    for d in range(1, Z):
        spread(d, False).wait_send()
    for d in range(Z):
        share(d, False).wait_send()

    def group(g):
        return image_ref[g // 2, g % 2]

    mine = group(rd).T
    for d in range(4):
        local[d * 128 : d * 128 + 128, :] = jnp.dot(
            mine, group(wrap(rd + d, 8)), precision=HIGHEST, preferred_element_type=jnp.float32
        )
    lower_half = rd % 4
    local[512:640, :] = jnp.dot(
        group(lower_half).T,
        group(lower_half + 4),
        precision=HIGHEST,
        preferred_element_type=jnp.float32,
    )

    @pl.when(rd >= 4)
    def _():
        local[512:576, :] = local[576:640, :]

    def sums(i, carry):
        numer, squares = carry
        old = panel_ref[pl.ds(pl.multiple_of(i * 8, 8), 8), :]
        new = jnp.concatenate(
            [image_ref[g // 2, g % 2, pl.ds(rd * ROWS + i, 1), :] for g in range(8)], axis=0
        )
        return numer + old * new, squares + old * old

    zero = jnp.zeros((8, 128), jnp.float32)
    numer, squares = lax.fori_loop(0, ROWS, sums, (zero, zero))
    local[576:584, :] = numer
    local[584:592, :] = squares
    local[592:640, :] = jnp.zeros((48, 128), jnp.float32)

    def to_y(d):
        where = pl.ds(pl.multiple_of(wrap(y + d, Y) * CHUNK, 8), CHUNK)
        return remote(
            local.at[where], from_y.at[d - 1], y_send.at[d - 1], y_recv.at[d - 1], y_peer(d)
        )

    for d in range(1, Y):
        to_y(d).start()
    for d in range(1, Y):
        to_y(d).wait()
    chunk = local[pl.ds(pl.multiple_of(y * CHUNK, 8), CHUNK), :]
    for d in range(Y - 1):
        chunk = chunk + from_y[d]
    total_y[...] = chunk
    from_x[x] = chunk

    def to_x(d, arrived):
        slot = wrap(x - d, X) if arrived else x
        return remote(
            total_y, from_x.at[slot], x_send.at[d - 1], x_recv.at[d - 1], x_peer(d)
        )

    for d in range(1, X):
        to_x(d, False).start()
    for d in range(1, X):
        to_x(d, True).wait_recv()
    for d in range(1, X):
        to_x(d, False).wait_send()
    total_x[...] = (from_x[0] + from_x[1]) + (from_x[2] + from_x[3])
    to_hi = remote(total_x, from_hi, h_send.at[0], h_recv.at[0], hi_peer)
    to_hi.start()
    to_hi.wait()
    here = pl.ds(pl.multiple_of(y * CHUNK, 8), CHUNK)
    parts_ref[z, core, here, :] = (total_x[...] + from_hi[...]) * (1.0 / N)

    def chunk_z(d, arrived):
        who = wrap(z - d, Z) if arrived else z
        where = parts_ref.at[who, core, here]
        return remote(where, where, c_send.at[d - 1], c_recv.at[d - 1], z_peer(d))

    for d in range(1, Z):
        chunk_z(d, False).start()
    for d in range(1, Z):
        chunk_z(d, True).wait_recv()
    for d in range(1, Z):
        chunk_z(d, False).wait_send()

    def gram_copy(key, arrived):
        kind, sign, at, first, count = GRAM_META[key]
        slot = GRAM_SLOT[key]
        side = core
        peer = core_peer
        if kind == "y":
            peer = y_peer(sign)
            at = at + sign if arrived else at
        elif arrived:
            side = 1 - core
        rows = pl.ds(pl.multiple_of(wrap(y - at % Y, Y) * CHUNK, 8), CHUNK)
        where = parts_ref.at[pl.ds(first, count), side, rows]
        return remote(where, where, g_send.at[slot], g_recv.at[slot], peer)

    for event, key in GRAM_EVENTS:
        if event == "start":
            gram_copy(key, False).start()
        else:
            gram_copy(key, True).wait_recv()
    for key in GRAM_MESSAGES:
        gram_copy(key, False).wait_send()


def combine(factor, panel):
    f32, bf16 = jnp.float32, jnp.bfloat16
    vmem = pl.BlockSpec(memory_space=pltpu.VMEM)

    def pair(n):
        return [pltpu.SemaphoreType.DMA((n,)), pltpu.SemaphoreType.DMA((n,))]

    return pl.pallas_call(
        combine_kernel,
        out_shape=(
            jax.ShapeDtypeStruct((Z, 2, BLOCK, 128), f32),
            jax.ShapeDtypeStruct((Z, 2, SLICE, 128), f32),
        ),
        in_specs=[vmem, vmem],
        out_specs=(vmem, vmem),
        scratch_shapes=[
            pltpu.VMEM((64 * SHARD, 128), f32),
            pltpu.VMEM((BLOCK, 8 * BLOCK), bf16),
            pltpu.VMEM((BLOCK, 8 * BLOCK), bf16),
            pltpu.VMEM((Z, 2, BLOCK, 128), f32),
            pltpu.VMEM((Z, BLOCK, 128), f32),
            pltpu.VMEM((Z - 1, BLOCK, 128), f32),
            pltpu.VMEM((SLICE, 128), f32),
            pltpu.VMEM((Y - 1, CHUNK, 128), f32),
            pltpu.VMEM((CHUNK, 128), f32),
            pltpu.VMEM((X, CHUNK, 128), f32),
            pltpu.VMEM((CHUNK, 128), f32),
            pltpu.VMEM((CHUNK, 128), f32),
            *pair(len(PANEL_MESSAGES)),
            *pair(Z),
            *pair(2 * Z),
            *pair(Y - 1),
            *pair(X - 1),
            *pair(1),
            *pair(Z - 1),
            *pair(len(GRAM_MESSAGES)),
        ],
        compiler_params=pltpu.CompilerParams(
            collective_id=0, has_side_effects=True, vmem_limit_bytes=50 << 20
        ),
        cost_estimate=pl.CostEstimate(
            flops=5 * 10**9, bytes_accessed=8 << 20, transcendentals=0
        ),
        name="combine",
    )(factor, panel)


def invert_block(a, out_ref):
    sub = lax.broadcasted_iota(jnp.int32, (8, 128), 0)
    lane = lax.broadcasted_iota(jnp.int32, (8, 128), 1)
    left = [a[8 * g:8 * g + 8, :] for g in range(16)]
    right = [jnp.where(lane == sub + 8 * g, 1.0, 0.0) for g in range(16)]
    def column(tile, at):
        return jnp.broadcast_to(tile[:, at:at + 1], (8, 128))
    def row(tile, at):
        return jnp.broadcast_to(tile[at:at + 1, :], (8, 128))
    for p in range(16):
        at, eye = left[p], right[p]
        cols = [column(at, 8 * p + k) for k in range(8)]
        heads, recips, pivots, marks = {}, [], [], []
        for k in range(8):
            d = row(cols[k], k)
            r = 1.0 / d
            m = jnp.where(sub > k, cols[k] * r, 0.0)
            u, w = row(at, k), row(eye, k)
            out_ref[8 * p + k:8 * p + k + 1, :] = (w * lax.rsqrt(d))[0:1, :]
            for c in range(k + 1, 8):
                heads[k, c] = row(cols[c], k)
                cols[c] = cols[c] - m * heads[k, c]
            at = at - m * u
            eye = eye - m * w
            recips.append(r); pivots.append(u); marks.append(w)
        for g in range(p + 1, 16):
            c_g = [column(left[g], 8 * p + k) for k in range(8)]
            lg, rg = left[g], right[g]
            for k in range(8):
                m = c_g[k] * recips[k]
                for c in range(k + 1, 8):
                    c_g[c] = c_g[c] - m * heads[k, c]
                lg = lg - m * pivots[k]
                rg = rg - m * marks[k]
            left[g], right[g] = lg, rg

def refresh_kernel(parts_ref, image_ref, panel_ref, values_ref, work, inverse, strip):
    num = sq = None
    for r in range(8):
        n_r = parts_ref[r * 640 + 576:r * 640 + 584, :]
        s_r = parts_ref[r * 640 + 584:r * 640 + 592, :]
        num = n_r if num is None else num + n_r
        sq = s_r if sq is None else sq + s_r
    values_ref[...] = num / (sq + 1e-06)
    for j in range(8):
        for i in range(j, 8):
            d = i - j
            if d == 4:
                block = jnp.concatenate([parts_ref[j * 640 + 512:j * 640 + 576, :], parts_ref[i * 640 + 512:i * 640 + 576, :]], axis=0).T
            elif d < 4:
                block = parts_ref[j * 640 + d * 128:j * 640 + d * 128 + 128, :]
                block = block.T if d else block
            else:
                block = parts_ref[i * 640 + (8 - d) * 128:i * 640 + (8 - d) * 128 + 128, :]
            work[j, i * 128:(i + 1) * 128, :] = block
        work[j, 1024:, :] = image_ref[j * 288:(j + 1) * 288, :]

    def step(j, carry):
        invert_block(work[j, pl.ds(pl.multiple_of(j * 128, 128), 128), :], inverse)
        for jj in range(8):
            @pl.when(j == jj)
            def _(jj=jj):
                top = (jj + 1) * 128
                strip[top:, :] = nt(work[jj, top:, :], inverse[...])
                panel_ref[:, jj * 128:(jj + 1) * 128] = strip[1024:, :]
                for k in range(jj + 1, 8):
                    work[k, k * 128:, :] -= nt(strip[k * 128:, :], strip[k * 128:(k + 1) * 128, :])
        return carry
    lax.fori_loop(0, 8, step, 0)

def refresh(parts, image):
    return pl.pallas_call(
        refresh_kernel,
        out_shape=(jax.ShapeDtypeStruct((288, 1024), jnp.float32), jax.ShapeDtypeStruct((8, 128), jnp.float32)),
        in_specs=[pl.BlockSpec(memory_space=pltpu.VMEM)] * 2,
        out_specs=(pl.BlockSpec(memory_space=pltpu.VMEM),) * 2,
        scratch_shapes=[pltpu.VMEM((8, 1312, 128), jnp.float32), pltpu.VMEM((128, 128), jnp.float32), pltpu.VMEM((1312, 128), jnp.float32)],
        compiler_params=pltpu.CompilerParams(vmem_limit_bytes=40 << 20),
        cost_estimate=pl.CostEstimate(flops=3 * 10**9, bytes_accessed=5 << 20, transcendentals=1024),
        name="refresh",
    )(parts, image)


def body(factor, panel):
    image, parts = combine(factor.reshape(BLOCK, 8 * BLOCK), panel.reshape(SHARD, 128))
    new_panel, values = refresh(
        parts.reshape(8 * SLICE, 128), image.reshape(8 * BLOCK, 128)
    )
    return (new_panel, values.reshape(1024))


def solution(mesh):
    placed = (P("blk", "rd", None), P(("blk", "rd"), None))
    return jax.shard_map(
        body, mesh=mesh, in_specs=placed, out_specs=(P("blk", None), P()), check_vma=False
    )
```

```python
import heapq

import jax
import jax.numpy as jnp
from jax import lax
from jax.experimental import pallas as pl
from jax.experimental.pallas import tpu as pltpu
from jax.sharding import PartitionSpec as P

N = 18432
X, Y, Z = 4, 8, 4
ROWS = 36
SHARD = ROWS * 8
BLOCK = 288
CHUNK = 80
SLICE = 8 * CHUNK
MESH = pl.DeviceIdType.MESH
HIGHEST = lax.Precision.HIGHEST


def ring(n):
    h = n // 2
    for sign in (1, -1):
        for t in range(h - 1):
            yield sign, sign * t, None
        yield sign, sign * (h - 1), 0 if sign > 0 else 1


def order(messages, preset=()):
    waiting = {k: set(m[3]) - set(preset) for k, m in messages.items()}
    followers = {}
    for k, m in messages.items():
        for d in m[3]:
            followers.setdefault(d, []).append(k)
    free, heap, events = {}, [], []

    def start(k, now):
        link, size, latency, _ = messages[k]
        begin = max(now, free.get(link, 0.0))
        free[link] = begin + size
        events.append(("start", k))
        heapq.heappush(heap, (begin + size + latency, len(events), k))

    for k in messages:
        if not waiting[k]:
            start(k, 0.0)
    while heap:
        now, _, k = heapq.heappop(heap)
        events.append(("wait", k))
        for f in followers.get(k, ()):
            waiting[f].discard(k)
            if not waiting[f]:
                start(f, now)
    assert sum(e == "start" for e, _ in events) == len(messages)
    return events


def panel_messages():
    rate = 50e3
    out = {}
    meta = {}
    z_key = ("z",)
    out[z_key] = ("z", SHARD * 512 / 25e3, 3.0, ())
    meta[z_key] = ("z", 0, 0, 0, 0, SHARD)
    for z in range(2):
        base = (z_key,) if z else ()
        for part, (first, rows) in enumerate(((0, 22), (22, 14))):
            axes = (("y", Y), ("x", X)) if part == 0 else (("x", X), ("y", Y))
            (f_name, f_n), (s_name, s_n) = axes
            half = rows // 2

            def cut(piece):
                return (first, rows) if piece is None else (first + piece * half, half)

            def offset(f, s):
                return (f, s) if f_name == "x" else (s, f)

            delivered = {0: base}
            for sign, at, piece in ring(f_n):
                key = (z, part, "f", 0, sign, at)
                dep = base if at == 0 else ((z, part, "f", 0, sign, at - sign),)
                start, count = cut(piece)
                ox, oy = offset(at, 0)
                out[key] = (f_name + str(sign), count * 4096 / rate, 1.0, dep)
                meta[key] = (f_name, sign, z, ox, oy, start * 8, count * 8)
                to = (at + sign) % f_n
                delivered[to] = delivered.get(to, ()) + (key,)
            for f in sorted(delivered, key=lambda v: min(v, f_n - v)):
                for sign, at, piece in ring(s_n):
                    key = (z, part, "s", f, sign, at)
                    dep = delivered[f] if at == 0 else ((z, part, "s", f, sign, at - sign),)
                    start, count = cut(piece)
                    ox, oy = offset(f, at)
                    out[key] = (s_name + str(sign), count * 4096 / rate, 1.0, dep)
                    meta[key] = (s_name, sign, z, ox, oy, start * 8, count * 8)
    return out, meta


def gram_messages():
    out = {}
    meta = {}
    delivered = {0: ()}
    for sign, at, piece in ring(Y):
        key = ("y", sign, at)
        dep = () if at == 0 else (("y", sign, at - sign),)
        first, count = (0, Z) if piece is None else (piece * Z // 2, Z // 2)
        out[key] = ("y" + str(sign), count * CHUNK * 512 / 50e3, 1.0, dep)
        meta[key] = ("y", sign, at, first, count)
        to = (at + sign) % Y
        delivered[to] = delivered.get(to, ()) + (key,)
    for f, dep in delivered.items():
        key = ("core", f)
        out[key] = ("core", Z * CHUNK * 512 / 400e3, 0.5, dep)
        meta[key] = ("core", 0, f, 0, Z)
    return out, meta


PANEL_MESSAGES, PANEL_META = panel_messages()
PANEL_EVENTS = order(PANEL_MESSAGES)
PANEL_SLOT = {k: i for i, k in enumerate(PANEL_MESSAGES)}
GRAM_MESSAGES, GRAM_META = gram_messages()
GRAM_EVENTS = order(GRAM_MESSAGES)
GRAM_SLOT = {k: i for i, k in enumerate(GRAM_MESSAGES)}


def combine_kernel(
    factor_ref,
    panel_ref,
    image_ref,
    parts_ref,
    gathered,
    high,
    low,
    partial,
    from_core,
    from_z,
    local,
    from_y,
    total_y,
    from_x,
    from_line,
    p_send,
    p_recv,
    r_send,
    r_recv,
    a_send,
    a_recv,
    y_send,
    y_recv,
    x_send,
    x_recv,
    h_send,
    h_recv,
    g_send,
    g_recv,
):
    blk = lax.axis_index("blk")
    rd = lax.axis_index("rd")
    hi, x, y = blk // (X * Y), (blk // Y) % X, blk % Y
    z, core = rd // 2, rd % 2

    def at_blk(h, i, j):
        return (h * X + i) * Y + j

    def wrap(v, n):
        return lax.rem(v + n, n)

    def x_peer(d):
        return (at_blk(hi, wrap(x + d, X), y), rd)

    def y_peer(d):
        return (at_blk(hi, x, wrap(y + d, Y)), rd)

    def z_peer(d):
        return (blk, wrap(z + d, Z) * 2 + core)

    def line_peer(d, e):
        return (at_blk(1 - hi if e else hi, x, y), wrap(z + d, Z) * 2 + core)

    hi_peer = line_peer(0, 1)
    core_peer = (blk, z * 2 + 1 - core)

    def remote(src, dst, send, recv, peer):
        return pltpu.make_async_remote_copy(
            src_ref=src,
            dst_ref=dst,
            send_sem=send,
            recv_sem=recv,
            device_id=peer,
            device_id_type=MESH,
        )

    barrier = pltpu.get_barrier_semaphore()
    peers = [x_peer(d) for d in range(1, X)] + [y_peer(d) for d in range(1, Y)]
    peers += [line_peer(d, e) for e in range(2) for d in range(1 - e, Z)] + [core_peer]
    for peer in peers:
        pl.semaphore_signal(barrier, inc=1, device_id=peer, device_id_type=MESH)

    own = pl.multiple_of(blk * SHARD, 8)
    gathered[pl.ds(own, SHARD), :] = panel_ref[...]
    pl.semaphore_wait(barrier, len(peers))

    def panel_copy(key, arrived):
        axis, sign, far, ox, oy, *span = PANEL_META[key]
        slot = PANEL_SLOT[key]
        if axis == "z":
            peer = hi_peer
            source = 1 - hi if arrived else hi
            start, count = 0, SHARD
            origin = at_blk(source, x, y)
        else:
            peer = x_peer(sign) if axis == "x" else y_peer(sign)
            start, count = span
            if arrived:
                ox, oy = (ox + sign, oy) if axis == "x" else (ox, oy + sign)
            source = 1 - hi if far else hi
            origin = at_blk(source, wrap(x - ox % X, X), wrap(y - oy % Y, Y))
        where = pl.ds(pl.multiple_of(origin * SHARD + start, 8), count)
        return remote(
            gathered.at[where], gathered.at[where], p_send.at[slot], p_recv.at[slot], peer
        )

    started = 0
    for event, key in PANEL_EVENTS:
        if event == "start":
            panel_copy(key, False).start()
        else:
            if started == 0:
                started = 1

                def split(i, carry):
                    rows = pl.ds(pl.multiple_of(i * 16, 16), 16)
                    value = factor_ref[rows, 0, :]
                    top = value.astype(jnp.bfloat16)
                    high[rows, :] = top
                    low[rows, :] = (value - top.astype(jnp.float32)).astype(jnp.bfloat16)
                    return carry

                lax.fori_loop(0, BLOCK // 16, split, 0)
            panel_copy(key, True).wait_recv()
    for key in PANEL_MESSAGES:
        panel_copy(key, False).wait_send()

    for q in range(4):
        right = jnp.concatenate(
            [gathered[pl.ds(2 * q + s, 8 * BLOCK, stride=8), :] for s in range(2)], axis=1
        )
        r_top = right.astype(jnp.bfloat16)
        r_low = (right - r_top.astype(jnp.float32)).astype(jnp.bfloat16)
        product = (
            jnp.dot(low[...], r_top, preferred_element_type=jnp.float32)
            + jnp.dot(high[...], r_low, preferred_element_type=jnp.float32)
            + jnp.dot(high[...], r_top, preferred_element_type=jnp.float32)
        )
        partial[q, 0] = product[:, :128]
        partial[q, 1] = product[:, 128:]

    to_core = remote(
        partial.at[:, 1 - core], from_core, r_send.at[0], r_recv.at[0], core_peer
    )
    to_core.start()
    to_core.wait()
    for k in range(Z):
        from_core[k] += partial[k, core]
    to_z = [
        remote(
            from_core.at[wrap(z + d, Z)],
            from_z.at[d - 1],
            r_send.at[d],
            r_recv.at[d],
            z_peer(d),
        )
        for d in range(1, Z)
    ]
    for copy in to_z:
        copy.start()
    for copy in to_z:
        copy.wait()
    image_ref[z, core] = from_core[z] + from_z[0] + from_z[1] + from_z[2]

    def spread(d, arrived):
        who = wrap(z - d, Z) if arrived else z
        where = image_ref.at[who, core]
        return remote(where, where, a_send.at[d], a_recv.at[d], z_peer(d))

    def share(k, arrived):
        who = wrap(z - k, Z)
        where = image_ref.at[who, 1 - core if arrived else core]
        return remote(where, where, a_send.at[Z + k], a_recv.at[Z + k], core_peer)

    for d in range(1, Z):
        spread(d, False).start()
    share(0, False).start()
    for d in range(1, Z):
        spread(d, True).wait_recv()
        share(d, False).start()
    for d in range(Z):
        share(d, True).wait_recv()
    for d in range(1, Z):
        spread(d, False).wait_send()
    for d in range(Z):
        share(d, False).wait_send()

    def group(g):
        return image_ref[g // 2, g % 2]

    mine = group(rd).T
    for d in range(4):
        local[d * 128 : d * 128 + 128, :] = jnp.dot(
            mine, group(wrap(rd + d, 8)), precision=HIGHEST, preferred_element_type=jnp.float32
        )
    lower_half = rd % 4
    local[512:640, :] = jnp.dot(
        group(lower_half).T,
        group(lower_half + 4),
        precision=HIGHEST,
        preferred_element_type=jnp.float32,
    )

    @pl.when(rd >= 4)
    def _():
        local[512:576, :] = local[576:640, :]

    for g in range(8):
        old = panel_ref[pl.ds(g, ROWS, stride=8), :]
        new = image_ref[g // 2, g % 2, pl.ds(rd * ROWS, ROWS), :]
        local[576 + g : 577 + g, :] = jnp.sum(old * new, axis=0, keepdims=True)
        local[584 + g : 585 + g, :] = jnp.sum(old * old, axis=0, keepdims=True)
    local[592:640, :] = jnp.zeros((48, 128), jnp.float32)

    def to_y(d):
        where = pl.ds(pl.multiple_of(wrap(y + d, Y) * CHUNK, 8), CHUNK)
        return remote(
            local.at[where], from_y.at[d - 1], y_send.at[d - 1], y_recv.at[d - 1], y_peer(d)
        )

    for d in range(1, Y):
        to_y(d).start()
    for d in range(1, Y):
        to_y(d).wait()
    chunk = local[pl.ds(pl.multiple_of(y * CHUNK, 8), CHUNK), :]
    for d in range(Y - 1):
        chunk = chunk + from_y[d]
    total_y[...] = chunk
    from_x[x] = chunk

    def to_x(d, arrived):
        slot = wrap(x - d, X) if arrived else x
        return remote(
            total_y, from_x.at[slot], x_send.at[d - 1], x_recv.at[d - 1], x_peer(d)
        )

    for d in range(1, X):
        to_x(d, False).start()
    for d in range(1, X):
        to_x(d, True).wait_recv()
    for d in range(1, X):
        to_x(d, False).wait_send()
    from_line[z, hi] = (from_x[0] + from_x[1]) + (from_x[2] + from_x[3])

    def to_line(d, e, arrived):
        from_hi = 1 - hi if e and arrived else hi
        where = from_line.at[wrap(z - d, Z) if arrived else z, from_hi]
        slot = 2 * d + e
        return remote(where, where, h_send.at[slot], h_recv.at[slot], line_peer(d, e))

    line = [(d, e) for d in (2, 1, 3, 0) for e in (1, 0) if d or e]
    for d, e in line:
        to_line(d, e, False).start()
    here = pl.ds(pl.multiple_of(y * CHUNK, 8), CHUNK)
    for d, e in line:
        to_line(d, e, True).wait_recv()
    for d, e in line:
        to_line(d, e, False).wait_send()
    for k in range(Z):
        parts_ref[k, core, here, :] = (from_line[k, 0] + from_line[k, 1]) * (1.0 / N)

    def gram_copy(key, arrived):
        kind, sign, at, first, count = GRAM_META[key]
        slot = GRAM_SLOT[key]
        side = core
        peer = core_peer
        if kind == "y":
            peer = y_peer(sign)
            at = at + sign if arrived else at
        elif arrived:
            side = 1 - core
        rows = pl.ds(pl.multiple_of(wrap(y - at % Y, Y) * CHUNK, 8), CHUNK)
        where = parts_ref.at[pl.ds(first, count), side, rows]
        return remote(where, where, g_send.at[slot], g_recv.at[slot], peer)

    for event, key in GRAM_EVENTS:
        if event == "start":
            gram_copy(key, False).start()
        else:
            gram_copy(key, True).wait_recv()
    for key in GRAM_MESSAGES:
        gram_copy(key, False).wait_send()


def combine(factor, panel):
    f32, bf16 = jnp.float32, jnp.bfloat16
    vmem = pl.BlockSpec(memory_space=pltpu.VMEM)

    def pair(n):
        return [pltpu.SemaphoreType.DMA((n,)), pltpu.SemaphoreType.DMA((n,))]

    return pl.pallas_call(
        combine_kernel,
        out_shape=(
            jax.ShapeDtypeStruct((Z, 2, BLOCK, 128), f32),
            jax.ShapeDtypeStruct((Z, 2, SLICE, 128), f32),
        ),
        in_specs=[vmem, vmem],
        out_specs=(vmem, vmem),
        scratch_shapes=[
            pltpu.VMEM((64 * SHARD, 128), f32),
            pltpu.VMEM((BLOCK, 8 * BLOCK), bf16),
            pltpu.VMEM((BLOCK, 8 * BLOCK), bf16),
            pltpu.VMEM((Z, 2, BLOCK, 128), f32),
            pltpu.VMEM((Z, BLOCK, 128), f32),
            pltpu.VMEM((Z - 1, BLOCK, 128), f32),
            pltpu.VMEM((SLICE, 128), f32),
            pltpu.VMEM((Y - 1, CHUNK, 128), f32),
            pltpu.VMEM((CHUNK, 128), f32),
            pltpu.VMEM((X, CHUNK, 128), f32),
            pltpu.VMEM((Z, 2, CHUNK, 128), f32),
            *pair(len(PANEL_MESSAGES)),
            *pair(Z),
            *pair(2 * Z),
            *pair(Y - 1),
            *pair(X - 1),
            *pair(2 * Z),
            *pair(len(GRAM_MESSAGES)),
        ],
        compiler_params=pltpu.CompilerParams(
            collective_id=0, has_side_effects=True, vmem_limit_bytes=50 << 20
        ),
        cost_estimate=pl.CostEstimate(
            flops=5 * 10**9, bytes_accessed=8 << 20, transcendentals=0
        ),
        name="combine",
    )(factor, panel)


def halves(value):
    top = value.astype(jnp.bfloat16)
    return top, (value - top.astype(jnp.float32)).astype(jnp.bfloat16)


def nt(a, b):
    def one(p, q):
        return lax.dot_general(
            p, q, (((1,), (1,)), ((), ())), preferred_element_type=jnp.float32
        )

    return one(a[1], b[0]) + one(a[0], b[1]) + one(a[0], b[0])


def invert_block(a, out_ref):
    sub = lax.broadcasted_iota(jnp.int32, (8, 128), 0)
    lane = lax.broadcasted_iota(jnp.int32, (8, 128), 1)
    left = [a[8 * g : 8 * g + 8, :] for g in range(16)]
    right = [jnp.where(lane == sub + 8 * g, 1.0, 0.0) for g in range(16)]

    def column(tile, at):
        return jnp.broadcast_to(tile[:, at : at + 1], (8, 128))

    def row(tile, at):
        return jnp.broadcast_to(tile[at : at + 1, :], (8, 128))

    for p in range(16):
        here, eye = left[p], right[p]
        cols = [column(here, 8 * p + k) for k in range(8)]
        heads, recips, pivots, marks = {}, [], [], []
        for k in range(8):
            d = row(cols[k], k)
            r = 1.0 / d
            m = jnp.where(sub > k, cols[k] * r, 0.0)
            u, w = row(here, k), row(eye, k)
            out_ref[8 * p + k : 8 * p + k + 1, :] = (w * lax.rsqrt(d))[0:1, :]
            for c in range(k + 1, 8):
                heads[k, c] = row(cols[c], k)
                cols[c] = cols[c] - m * heads[k, c]
            here = here - m * u
            eye = eye - m * w
            recips.append(r)
            pivots.append(u)
            marks.append(w)
        for g in range(p + 1, 16):
            tall = [column(left[g], 8 * p + k) for k in range(8)]
            lg, rg = left[g], right[g]
            for k in range(8):
                m = tall[k] * recips[k]
                for c in range(k + 1, 8):
                    tall[c] = tall[c] - m * heads[k, c]
                lg = lg - m * pivots[k]
                rg = rg - m * marks[k]
            left[g], right[g] = lg, rg


TALL = 1024 + BLOCK
PIECE = TALL // 4


def refresh_kernel(
    parts_ref, image_ref, panel_ref, values_ref, work, rest, high, low, inverse, w_high, w_low
):
    num = sq = None
    for r in range(8):
        at = r * SLICE + 576
        n_r, s_r = parts_ref[at : at + 8, :], parts_ref[at + 8 : at + 16, :]
        num = n_r if num is None else num + n_r
        sq = s_r if sq is None else sq + s_r
    values_ref[...] = num / (sq + 1e-06)
    for j in range(8):
        for i in range(j, 8):
            d, at, far = i - j, j * SLICE, i * SLICE
            if d == 4:
                block = jnp.concatenate(
                    [parts_ref[at + 512 : at + 576, :], parts_ref[far + 512 : far + 576, :]],
                    axis=0,
                ).T
            elif d < 4:
                block = parts_ref[at + d * 128 : at + d * 128 + 128, :]
                block = block.T if d else block
            else:
                block = parts_ref[far + (8 - d) * 128 : far + (8 - d) * 128 + 128, :]
            work[j, i * 128 : (i + 1) * 128, :] = block
        work[j, 1024:, :] = image_ref[j * BLOCK : (j + 1) * BLOCK, :]
    high[...] = jnp.zeros_like(high)
    low[...] = jnp.zeros_like(low)
    rest[...] = jnp.zeros_like(rest)
    inverse[...] = jnp.zeros_like(inverse)

    def step(j, carry):
        done = pl.ds(pl.multiple_of(jnp.maximum(j - 1, 0) * 128, 128), 128)
        rows = pl.ds(pl.multiple_of(j * 128, 128), 128)
        before = halves(inverse[...])
        w_high[...], w_low[...] = before
        strip = halves(nt(halves(rest[rows, :]), before))
        high[rows, done], low[rows, done] = strip
        side = (high[rows, :], low[rows, :])
        invert_block(work[j, rows, :] - nt(side, side), inverse)
        for n in range(4):
            span = slice(n * PIECE, (n + 1) * PIECE)
            solved = nt(halves(rest[span, :]), (w_high[...], w_low[...]))
            if n == 3:
                panel_ref[:, done] = solved[PIECE - BLOCK :, :]
            high[span, done], low[span, done] = halves(solved)
            rest[span, :] = work[j, span, :] - nt((high[span, :], low[span, :]), side)
        return carry

    lax.fori_loop(0, 8, step, 0)
    panel_ref[:, 896:] = nt(halves(rest[1024:, :]), halves(inverse[...]))


def refresh(parts, image):
    f32, bf16 = jnp.float32, jnp.bfloat16
    vmem = pl.BlockSpec(memory_space=pltpu.VMEM)
    return pl.pallas_call(
        refresh_kernel,
        out_shape=(
            jax.ShapeDtypeStruct((BLOCK, 1024), f32),
            jax.ShapeDtypeStruct((8, 128), f32),
        ),
        in_specs=[vmem, vmem],
        out_specs=(vmem, vmem),
        scratch_shapes=[
            pltpu.VMEM((8, TALL, 128), f32),
            pltpu.VMEM((TALL, 128), f32),
            pltpu.VMEM((TALL, 1024), bf16),
            pltpu.VMEM((TALL, 1024), bf16),
            pltpu.VMEM((128, 128), f32),
            pltpu.VMEM((128, 128), bf16),
            pltpu.VMEM((128, 128), bf16),
        ],
        compiler_params=pltpu.CompilerParams(vmem_limit_bytes=48 << 20),
        cost_estimate=pl.CostEstimate(
            flops=3 * 10**9, bytes_accessed=5 << 20, transcendentals=1024
        ),
        name="refresh",
    )(parts, image)


def body(factor, panel):
    image, parts = combine(factor, panel.reshape(SHARD, 128))
    new_panel, values = refresh(
        parts.reshape(8 * SLICE, 128), image.reshape(8 * BLOCK, 128)
    )
    return (new_panel, values.reshape(1024))


def solution(mesh):
    placed = (P("blk", "rd", None), P(("blk", "rd"), None))
    return jax.shard_map(
        body, mesh=mesh, in_specs=placed, out_specs=(P("blk", None), P()), check_vma=False
    )
```

```python
import heapq

import jax
import jax.numpy as jnp
from jax import lax
from jax.experimental import pallas as pl
from jax.experimental.pallas import tpu as pltpu
from jax.sharding import PartitionSpec as P

N = 18432
X, Y, Z = 4, 8, 4
ROWS = 36
HALF = ROWS * 4
SIDE = X * Y * HALF
BLOCK = 288
CHUNK = 80
SLICE = 8 * CHUNK
MESH = pl.DeviceIdType.MESH
HIGHEST = lax.Precision.HIGHEST


def ring(n, whole=0):
    h = n // 2
    for sign in (1, -1):
        for t in range(h - 1):
            yield sign, sign * t, None
        if whole == 0:
            yield sign, sign * (h - 1), 0 if sign > 0 else 1
        elif whole == sign:
            yield sign, sign * (h - 1), None


def order(nodes, ahead=2.0):
    waiting = {k: set(v[3]) for k, v in nodes.items()}
    followers = {}
    for k, v in nodes.items():
        for d in set(v[3]):
            followers.setdefault(d, []).append(k)
    free, queues, heap, events = {}, {}, [], []
    place = {k: i for i, k in enumerate(nodes)}

    def push(when, kind, what):
        push.count += 1
        heapq.heappush(heap, (when, push.count, kind, what))

    push.count = 0

    def pump(resource, now):
        queue = queues.setdefault(resource, [])
        reach = 0.0 if resource == "tc" else ahead
        while queue and free.get(resource, 0.0) - now <= reach:
            key = heapq.heappop(queue)[2]
            begin = max(now, free.get(resource, 0.0))
            free[resource] = begin + nodes[key][1]
            events.append(("task" if resource == "tc" else "start", key))
            push(free[resource] + nodes[key][2], "done", key)
        if queue:
            push(free[resource] - reach, "pump", resource)

    def ready(key, now):
        heapq.heappush(queues.setdefault(nodes[key][0], []), (nodes[key][4], place[key], key))
        pump(nodes[key][0], now)

    for k in nodes:
        if not waiting[k]:
            ready(k, 0.0)
    while heap:
        now, _, kind, what = heapq.heappop(heap)
        if kind == "pump":
            pump(what, now)
            continue
        if nodes[what][0] != "tc":
            events.append(("wait", what))
        for f in followers.get(what, ()):
            waiting[f].discard(what)
            if not waiting[f]:
                ready(f, now)
    assert not any(waiting.values())
    return events


SPLITS = 6


def image_nodes():
    rate = 50e3
    out, meta = {}, {}
    splits = tuple(("split", i) for i in range(SPLITS))
    products = {0: [], 1: []}
    early = []
    for unit, (h, far) in enumerate(((0, 0), (0, 1), (1, 2))):
        needs = ()
        if far:
            z_key = ("hi", h)
            out[z_key] = ("z", HALF * 1024 / 50e3, 3.0, (), h)
            meta[z_key] = ("hi", h, 0, 0, 0, 0, 0, HALF)
            needs = (z_key,)
        wide = 2 if far == 2 else 1
        arrivals = []
        for part, (first, rows) in enumerate(((0, 22), (22, 14))):
            axes = (("y", Y), ("x", X)) if part == 0 else (("x", X), ("y", Y))
            (f_name, f_n), (s_name, s_n) = axes
            big = (rows // 2 + 1) // 2 * 2

            def cut(piece):
                if piece is None:
                    return first, rows
                return (first, big) if piece == 0 else (first + big, rows - big)

            def send(key, name, sign, f, s, piece, dep):
                start, count = cut(piece)
                ox, oy = (f, s) if f_name == "x" else (s, f)
                took = count * 4 * 512 * wide / rate
                out[key] = (name + str(sign), took, 1.0, dep, 2 * unit + (key[3] != "f"))
                meta[key] = (name, h, far, sign, ox, oy, start * 4, count * 4)
                arrivals.append(key)

            delivered = {0: needs}
            for sign, at, piece in ring(f_n):
                key = (unit, part, sign, "f", 0, at)
                dep = needs if at == 0 else ((unit, part, sign, "f", 0, at - sign),)
                send(key, f_name, sign, at, 0, piece, dep)
                to = (at + sign) % f_n
                delivered[to] = delivered.get(to, ()) + (key,)
            for f in sorted(delivered, key=lambda v: min(v, f_n - v)):
                for sign, at, piece in ring(s_n, 1 if f % 2 == 0 else -1):
                    key = (unit, part, sign, "s", f, at)
                    dep = (
                        delivered[f] if at == 0 else ((unit, part, sign, "s", f, at - sign),)
                    )
                    send(key, s_name, sign, f, at, piece, dep)
        if unit == 0:
            early = arrivals
        for side in (far,) if far < 2 else (0, 1):
            for q in range(2):
                key = ("product", h, side, q)
                out[key] = ("tc", 0.8, 0.0, needs + tuple(arrivals) + splits, 0)
                products[h].append(key)
    for i, key in enumerate(splits):
        out[key] = ("tc", 0.5, 0.0, (early[4 + 6 * i],), 1)
    for h in range(2):
        out["core", h] = ("c", 0.7, 1.0, tuple(products[h]), 0)
        out["add", h] = ("tc", 0.3, 0.0, (("core", h),), 0)
        out["own", h] = ("tc", 0.2, 0.0, tuple(("sum", h, d) for d in range(1, Z)), 0)
        for d in (2, 1, 3):
            out["sum", h, d] = ("zz", 2.0, 1.5, (("add", h),), 0)
            out["spread", h, d] = ("zz", 2.0, 1.5, (("own", h),), 0)
        for d in range(Z):
            dep = ("spread", h, d) if d else ("own", h)
            out["share", h, d] = ("c", 0.2, 0.7, (dep,), 0)
    for key in out:
        if key not in meta and out[key][0] != "tc":
            meta[key] = key
    return out, meta


def gram_messages():
    out = {}
    meta = {}
    delivered = {0: ()}
    for sign, at, piece in ring(Y):
        key = ("y", sign, at)
        dep = () if at == 0 else (("y", sign, at - sign),)
        first, count = (0, Z) if piece is None else (piece * Z // 2, Z // 2)
        out[key] = ("y" + str(sign), count * CHUNK * 512 / 50e3, 1.0, dep, 0)
        meta[key] = ("y", sign, at, first, count)
        to = (at + sign) % Y
        delivered[to] = delivered.get(to, ()) + (key,)
    for f, dep in delivered.items():
        key = ("core", f)
        out[key] = ("core", Z * CHUNK * 512 / 400e3, 0.5, dep, 0)
        meta[key] = ("core", 0, f, 0, Z)
    return out, meta


IMAGE_NODES, IMAGE_META = image_nodes()
IMAGE_EVENTS = order(IMAGE_NODES)
IMAGE_SLOT = {k: i for i, k in enumerate(IMAGE_META)}
GRAM_MESSAGES, GRAM_META = gram_messages()
GRAM_EVENTS = order(GRAM_MESSAGES)
GRAM_SLOT = {k: i for i, k in enumerate(GRAM_MESSAGES)}


def combine_kernel(
    factor_ref,
    panel_ref,
    image_ref,
    parts_ref,
    gathered,
    high,
    low,
    partial,
    from_core,
    from_z,
    local,
    from_y,
    total_y,
    from_x,
    from_line,
    p_send,
    p_recv,
    y_send,
    y_recv,
    x_send,
    x_recv,
    h_send,
    h_recv,
    g_send,
    g_recv,
):
    blk = lax.axis_index("blk")
    rd = lax.axis_index("rd")
    hi, x, y = blk // (X * Y), (blk // Y) % X, blk % Y
    z, core = rd // 2, rd % 2

    def at_blk(h, i, j):
        return (h * X + i) * Y + j

    def wrap(v, n):
        return lax.rem(v + n, n)

    def x_peer(d):
        return (at_blk(hi, wrap(x + d, X), y), rd)

    def y_peer(d):
        return (at_blk(hi, x, wrap(y + d, Y)), rd)

    def z_peer(d):
        return (blk, wrap(z + d, Z) * 2 + core)

    def line_peer(d, e):
        return (at_blk(1 - hi if e else hi, x, y), wrap(z + d, Z) * 2 + core)

    hi_peer = line_peer(0, 1)
    core_peer = (blk, z * 2 + 1 - core)

    def remote(src, dst, send, recv, peer):
        return pltpu.make_async_remote_copy(
            src_ref=src,
            dst_ref=dst,
            send_sem=send,
            recv_sem=recv,
            device_id=peer,
            device_id_type=MESH,
        )

    barrier = pltpu.get_barrier_semaphore()
    peers = [x_peer(d) for d in range(1, X)] + [y_peer(d) for d in range(1, Y)]
    peers += [line_peer(d, e) for e in range(2) for d in range(1 - e, Z)] + [core_peer]
    for peer in peers:
        pl.semaphore_signal(barrier, inc=1, device_id=peer, device_id_type=MESH)

    own = pl.ds(pl.multiple_of((x * Y + y) * HALF, 8), HALF)
    for h in range(2):
        gathered[h, hi, own, :] = panel_ref[h]
    pl.semaphore_wait(barrier, len(peers))

    my_rows = pl.ds(pl.multiple_of(core * (BLOCK // 2), 8), BLOCK // 2)
    other_rows = pl.ds(pl.multiple_of((1 - core) * (BLOCK // 2), 8), BLOCK // 2)

    def image_copy(key, arrived):
        kind, h, *more = IMAGE_META[key]
        if kind in ("x", "y", "hi"):
            far, sign, ox, oy, start, count = more
            if kind == "hi":
                peer = hi_peer
                side = 1 - hi if arrived else hi
            else:
                peer = x_peer(sign) if kind == "x" else y_peer(sign)
                side = (hi, 1 - hi, slice(None))[far]
                if arrived:
                    ox, oy = (ox + sign, oy) if kind == "x" else (ox, oy + sign)
            origin = wrap(x - ox % X, X) * Y + wrap(y - oy % Y, Y)
            rows = pl.ds(pl.multiple_of(origin * HALF + start, 8), count)
            src = dst = gathered.at[h, side, rows]
        elif kind == "core":
            peer = core_peer
            src, dst = partial.at[h, :, other_rows], from_core.at[h]
        elif kind == "sum":
            d = more[0]
            peer = z_peer(d)
            src, dst = from_core.at[h, wrap(z + d, Z)], from_z.at[h, d - 1]
        elif kind == "spread":
            d = more[0]
            peer = z_peer(d)
            src = dst = image_ref.at[4 * h + (wrap(z - d, Z) if arrived else z), my_rows]
        else:
            d = more[0]
            peer = core_peer
            rows = other_rows if arrived else my_rows
            src = dst = image_ref.at[4 * h + wrap(z - d, Z), rows]
        slot = IMAGE_SLOT[key]
        return remote(src, dst, p_send.at[slot], p_recv.at[slot], peer)

    def split(i):
        count = BLOCK // SPLITS
        rows = slice(i * count, (i + 1) * count)
        value = factor_ref[rows, 0, :]
        high[rows, :], low[rows, :] = halves(value)

    def product(h, far, q):
        side = 1 - hi if far else hi
        right = jnp.concatenate(
            [gathered[h, side, pl.ds(2 * q + s, SIDE // 4, stride=4), :] for s in range(2)],
            axis=1,
        )
        top, rest = halves(right)
        span = pl.ds(pl.multiple_of(side * (SIDE // 4), 128), SIDE // 4)
        value = (
            jnp.dot(low[:, span], top, preferred_element_type=jnp.float32)
            + jnp.dot(high[:, span], rest, preferred_element_type=jnp.float32)
            + jnp.dot(high[:, span], top, preferred_element_type=jnp.float32)
        )
        for s in range(2):
            piece = value[:, s * 128 : s * 128 + 128]
            if far:
                piece = partial[h, 2 * q + s] + piece
            partial[h, 2 * q + s] = piece

    def add(h):
        for k in range(Z):
            from_core[h, k] += partial[h, k, my_rows, :]

    def own_sum(h):
        value = from_core[h, z] + from_z[h, 0] + from_z[h, 1] + from_z[h, 2]
        image_ref[4 * h + z, my_rows, :] = value

    tasks = dict(split=split, product=product, add=add, own=own_sum)
    for event, key in IMAGE_EVENTS:
        if event == "start":
            image_copy(key, False).start()
        elif event == "wait":
            image_copy(key, True).wait_recv()
        else:
            tasks[key[0]](*key[1:])
    for key in IMAGE_META:
        image_copy(key, False).wait_send()

    def group(g):
        return image_ref[g]

    mine = group(rd).T
    for d in range(4):
        local[d * 128 : d * 128 + 128, :] = jnp.dot(
            mine, group(wrap(rd + d, 8)), precision=HIGHEST, preferred_element_type=jnp.float32
        )
    lower_half = rd % 4
    local[512:640, :] = jnp.dot(
        group(lower_half).T,
        group(lower_half + 4),
        precision=HIGHEST,
        preferred_element_type=jnp.float32,
    )

    @pl.when(rd >= 4)
    def _():
        local[512:576, :] = local[576:640, :]

    for g in range(8):
        old = panel_ref[g // 4, pl.ds(g % 4, ROWS, stride=4), :]
        new = image_ref[g, pl.ds(rd * ROWS, ROWS), :]
        local[576 + g : 577 + g, :] = jnp.sum(old * new, axis=0, keepdims=True)
        local[584 + g : 585 + g, :] = jnp.sum(old * old, axis=0, keepdims=True)
    local[592:640, :] = jnp.zeros((48, 128), jnp.float32)

    def to_y(d):
        where = pl.ds(pl.multiple_of(wrap(y + d, Y) * CHUNK, 8), CHUNK)
        return remote(
            local.at[where], from_y.at[d - 1], y_send.at[d - 1], y_recv.at[d - 1], y_peer(d)
        )

    for d in range(1, Y):
        to_y(d).start()
    for d in range(1, Y):
        to_y(d).wait()
    chunk = local[pl.ds(pl.multiple_of(y * CHUNK, 8), CHUNK), :]
    for d in range(Y - 1):
        chunk = chunk + from_y[d]
    total_y[...] = chunk
    from_x[x] = chunk

    def to_x(d, arrived):
        slot = wrap(x - d, X) if arrived else x
        return remote(
            total_y, from_x.at[slot], x_send.at[d - 1], x_recv.at[d - 1], x_peer(d)
        )

    for d in range(1, X):
        to_x(d, False).start()
    for d in range(1, X):
        to_x(d, True).wait_recv()
    for d in range(1, X):
        to_x(d, False).wait_send()
    from_line[z, hi] = (from_x[0] + from_x[1]) + (from_x[2] + from_x[3])

    def to_line(d, e, arrived):
        from_hi = 1 - hi if e and arrived else hi
        where = from_line.at[wrap(z - d, Z) if arrived else z, from_hi]
        slot = 2 * d + e
        return remote(where, where, h_send.at[slot], h_recv.at[slot], line_peer(d, e))

    line = [(d, e) for d in (2, 1, 3, 0) for e in (1, 0) if d or e]
    for d, e in line:
        to_line(d, e, False).start()
    here = pl.ds(pl.multiple_of(y * CHUNK, 8), CHUNK)
    for d, e in line:
        to_line(d, e, True).wait_recv()
    for d, e in line:
        to_line(d, e, False).wait_send()
    for k in range(Z):
        parts_ref[k, core, here, :] = (from_line[k, 0] + from_line[k, 1]) * (1.0 / N)

    def gram_copy(key, arrived):
        kind, sign, at, first, count = GRAM_META[key]
        slot = GRAM_SLOT[key]
        side = core
        peer = core_peer
        if kind == "y":
            peer = y_peer(sign)
            at = at + sign if arrived else at
        elif arrived:
            side = 1 - core
        rows = pl.ds(pl.multiple_of(wrap(y - at % Y, Y) * CHUNK, 8), CHUNK)
        where = parts_ref.at[pl.ds(first, count), side, rows]
        return remote(where, where, g_send.at[slot], g_recv.at[slot], peer)

    for event, key in GRAM_EVENTS:
        if event == "start":
            gram_copy(key, False).start()
        else:
            gram_copy(key, True).wait_recv()
    for key in GRAM_MESSAGES:
        gram_copy(key, False).wait_send()


def combine(factor, panel):
    f32, bf16 = jnp.float32, jnp.bfloat16
    vmem = pl.BlockSpec(memory_space=pltpu.VMEM)

    def pair(n):
        return [pltpu.SemaphoreType.DMA((n,)), pltpu.SemaphoreType.DMA((n,))]

    return pl.pallas_call(
        combine_kernel,
        out_shape=(
            jax.ShapeDtypeStruct((8, BLOCK, 128), f32),
            jax.ShapeDtypeStruct((Z, 2, SLICE, 128), f32),
        ),
        in_specs=[vmem, vmem],
        out_specs=(vmem, vmem),
        scratch_shapes=[
            pltpu.VMEM((2, 2, SIDE, 128), f32),
            pltpu.VMEM((BLOCK, 8 * BLOCK), bf16),
            pltpu.VMEM((BLOCK, 8 * BLOCK), bf16),
            pltpu.VMEM((2, Z, BLOCK, 128), f32),
            pltpu.VMEM((2, Z, BLOCK // 2, 128), f32),
            pltpu.VMEM((2, Z - 1, BLOCK // 2, 128), f32),
            pltpu.VMEM((SLICE, 128), f32),
            pltpu.VMEM((Y - 1, CHUNK, 128), f32),
            pltpu.VMEM((CHUNK, 128), f32),
            pltpu.VMEM((X, CHUNK, 128), f32),
            pltpu.VMEM((Z, 2, CHUNK, 128), f32),
            *pair(len(IMAGE_META)),
            *pair(Y - 1),
            *pair(X - 1),
            *pair(2 * Z),
            *pair(len(GRAM_MESSAGES)),
        ],
        compiler_params=pltpu.CompilerParams(
            collective_id=0, has_side_effects=True, vmem_limit_bytes=50 << 20
        ),
        cost_estimate=pl.CostEstimate(
            flops=5 * 10**9, bytes_accessed=8 << 20, transcendentals=0
        ),
        name="combine",
    )(factor, panel)


def halves(value):
    top = value.astype(jnp.bfloat16)
    return top, (value - top.astype(jnp.float32)).astype(jnp.bfloat16)


def nt(a, b):
    def one(p, q):
        return lax.dot_general(
            p, q, (((1,), (1,)), ((), ())), preferred_element_type=jnp.float32
        )

    return one(a[1], b[0]) + one(a[0], b[1]) + one(a[0], b[0])


def invert_block(a, out_ref):
    sub = lax.broadcasted_iota(jnp.int32, (8, 128), 0)
    lane = lax.broadcasted_iota(jnp.int32, (8, 128), 1)
    left = [a[8 * g : 8 * g + 8, :] for g in range(16)]
    right = [jnp.where(lane == sub + 8 * g, 1.0, 0.0) for g in range(16)]

    def column(tile, at):
        return jnp.broadcast_to(tile[:, at : at + 1], (8, 128))

    def row(tile, at):
        return jnp.broadcast_to(tile[at : at + 1, :], (8, 128))

    for p in range(16):
        here, eye = left[p], right[p]
        cols = [column(here, 8 * p + k) for k in range(8)]
        heads, recips, pivots, marks = {}, [], [], []
        for k in range(8):
            d = row(cols[k], k)
            r = 1.0 / d
            m = jnp.where(sub > k, cols[k] * r, 0.0)
            u, w = row(here, k), row(eye, k)
            out_ref[8 * p + k : 8 * p + k + 1, :] = (w * lax.rsqrt(d))[0:1, :]
            for c in range(k + 1, 8):
                heads[k, c] = row(cols[c], k)
                cols[c] = cols[c] - m * heads[k, c]
            here = here - m * u
            eye = eye - m * w
            recips.append(r)
            pivots.append(u)
            marks.append(w)
        for g in range(p + 1, 16):
            tall = [column(left[g], 8 * p + k) for k in range(8)]
            lg, rg = left[g], right[g]
            for k in range(8):
                m = tall[k] * recips[k]
                for c in range(k + 1, 8):
                    tall[c] = tall[c] - m * heads[k, c]
                lg = lg - m * pivots[k]
                rg = rg - m * marks[k]
            left[g], right[g] = lg, rg


TALL = 1024 + BLOCK
PIECE = TALL // 4


def refresh_kernel(
    parts_ref, image_ref, panel_ref, values_ref, work, rest, high, low, inverse, w_high, w_low
):
    num = sq = None
    for r in range(8):
        at = r * SLICE + 576
        n_r, s_r = parts_ref[at : at + 8, :], parts_ref[at + 8 : at + 16, :]
        num = n_r if num is None else num + n_r
        sq = s_r if sq is None else sq + s_r
    values_ref[...] = num / (sq + 1e-06)
    for j in range(8):
        for i in range(j, 8):
            d, at, far = i - j, j * SLICE, i * SLICE
            if d == 4:
                block = jnp.concatenate(
                    [parts_ref[at + 512 : at + 576, :], parts_ref[far + 512 : far + 576, :]],
                    axis=0,
                ).T
            elif d < 4:
                block = parts_ref[at + d * 128 : at + d * 128 + 128, :]
                block = block.T if d else block
            else:
                block = parts_ref[far + (8 - d) * 128 : far + (8 - d) * 128 + 128, :]
            work[j, i * 128 : (i + 1) * 128, :] = block
        work[j, 1024:, :] = image_ref[j * BLOCK : (j + 1) * BLOCK, :]
    high[...] = jnp.zeros_like(high)
    low[...] = jnp.zeros_like(low)
    rest[...] = jnp.zeros_like(rest)
    inverse[...] = jnp.zeros_like(inverse)

    def step(j, carry):
        done = pl.ds(pl.multiple_of(jnp.maximum(j - 1, 0) * 128, 128), 128)
        rows = pl.ds(pl.multiple_of(j * 128, 128), 128)
        before = halves(inverse[...])
        w_high[...], w_low[...] = before
        strip = halves(nt(halves(rest[rows, :]), before))
        high[rows, done], low[rows, done] = strip
        side = (high[rows, :], low[rows, :])
        invert_block(work[j, rows, :] - nt(side, side), inverse)
        for n in range(4):
            span = slice(n * PIECE, (n + 1) * PIECE)
            solved = nt(halves(rest[span, :]), (w_high[...], w_low[...]))
            if n == 3:
                panel_ref[:, done] = solved[PIECE - BLOCK :, :]
            high[span, done], low[span, done] = halves(solved)
            rest[span, :] = work[j, span, :] - nt((high[span, :], low[span, :]), side)
        return carry

    lax.fori_loop(0, 8, step, 0)
    panel_ref[:, 896:] = nt(halves(rest[1024:, :]), halves(inverse[...]))


def refresh(parts, image):
    f32, bf16 = jnp.float32, jnp.bfloat16
    vmem = pl.BlockSpec(memory_space=pltpu.VMEM)
    return pl.pallas_call(
        refresh_kernel,
        out_shape=(
            jax.ShapeDtypeStruct((BLOCK, 1024), f32),
            jax.ShapeDtypeStruct((8, 128), f32),
        ),
        in_specs=[vmem, vmem],
        out_specs=(vmem, vmem),
        scratch_shapes=[
            pltpu.VMEM((8, TALL, 128), f32),
            pltpu.VMEM((TALL, 128), f32),
            pltpu.VMEM((TALL, 1024), bf16),
            pltpu.VMEM((TALL, 1024), bf16),
            pltpu.VMEM((128, 128), f32),
            pltpu.VMEM((128, 128), bf16),
            pltpu.VMEM((128, 128), bf16),
        ],
        compiler_params=pltpu.CompilerParams(vmem_limit_bytes=48 << 20),
        cost_estimate=pl.CostEstimate(
            flops=3 * 10**9, bytes_accessed=5 << 20, transcendentals=1024
        ),
        name="refresh",
    )(parts, image)


def body(factor, panel):
    image, parts = combine(
        factor, panel.reshape(ROWS, 2, 4, 128).transpose(1, 0, 2, 3).reshape(2, HALF, 128)
    )
    new_panel, values = refresh(
        parts.reshape(8 * SLICE, 128), image.reshape(8 * BLOCK, 128)
    )
    return (new_panel, values.reshape(1024))


def solution(mesh):
    placed = (P("blk", "rd", None), P(("blk", "rd"), None))
    return jax.shard_map(
        body, mesh=mesh, in_specs=placed, out_specs=(P("blk", None), P()), check_vma=False
    )
```

```python
import heapq

import jax
import jax.numpy as jnp
from jax import lax
from jax.experimental import pallas as pl
from jax.experimental.pallas import tpu as pltpu
from jax.sharding import PartitionSpec as P

N = 18432
X, Y, Z = 4, 8, 4
ROWS = 36
HALF = ROWS * 4
SIDE = X * Y * HALF
BLOCK = 288
CHUNK = 24
SLICE = X * Y * CHUNK
X_ROWS = Y * CHUNK
MESH = pl.DeviceIdType.MESH
HIGHEST = lax.Precision.HIGHEST


def ring(n, whole=0):
    h = n // 2
    for sign in (1, -1):
        for t in range(h - 1):
            yield sign, sign * t, None
        if whole == 0:
            yield sign, sign * (h - 1), 0 if sign > 0 else 1
        elif whole == sign:
            yield sign, sign * (h - 1), None


def order(nodes, ahead=2.0):
    waiting = {k: set(v[3]) for k, v in nodes.items()}
    followers = {}
    for k, v in nodes.items():
        for d in set(v[3]):
            followers.setdefault(d, []).append(k)
    free, queues, heap, events = {}, {}, [], []
    place = {k: i for i, k in enumerate(nodes)}

    def push(when, kind, what):
        push.count += 1
        heapq.heappush(heap, (when, push.count, kind, what))

    push.count = 0

    def pump(resource, now):
        queue = queues.setdefault(resource, [])
        reach = 0.0 if resource == "tc" else ahead
        while queue and free.get(resource, 0.0) - now <= reach:
            key = heapq.heappop(queue)[2]
            begin = max(now, free.get(resource, 0.0))
            free[resource] = begin + nodes[key][1]
            events.append(("task" if resource == "tc" else "start", key))
            push(free[resource] + nodes[key][2], "done", key)
        if queue:
            push(free[resource] - reach, "pump", resource)

    def ready(key, now):
        heapq.heappush(queues.setdefault(nodes[key][0], []), (nodes[key][4], place[key], key))
        pump(nodes[key][0], now)

    for k in nodes:
        if not waiting[k]:
            ready(k, 0.0)
    while heap:
        now, _, kind, what = heapq.heappop(heap)
        if kind == "pump":
            pump(what, now)
            continue
        if nodes[what][0] != "tc":
            events.append(("wait", what))
        for f in followers.get(what, ()):
            waiting[f].discard(what)
            if not waiting[f]:
                ready(f, now)
    assert not any(waiting.values())
    return events


SPLITS = 6


def image_nodes():
    rate = 50e3
    out, meta = {}, {}
    splits = tuple(("split", i) for i in range(SPLITS))
    products = {0: [], 1: []}
    early = []
    for unit, (h, far) in enumerate(((0, 0), (0, 1), (1, 2))):
        needs = ()
        if far:
            z_key = ("hi", h)
            out[z_key] = ("z", HALF * 1024 / 50e3, 3.0, (), h)
            meta[z_key] = ("hi", h, 0, 0, 0, 0, 0, HALF)
            needs = (z_key,)
        wide = 2 if far == 2 else 1
        arrivals = []
        for part, (first, rows) in enumerate(((0, 22), (22, 14))):
            axes = (("y", Y), ("x", X)) if part == 0 else (("x", X), ("y", Y))
            (f_name, f_n), (s_name, s_n) = axes
            big = (rows // 2 + 1) // 2 * 2

            def cut(piece):
                if piece is None:
                    return first, rows
                return (first, big) if piece == 0 else (first + big, rows - big)

            def send(key, name, sign, f, s, piece, dep):
                start, count = cut(piece)
                ox, oy = (f, s) if f_name == "x" else (s, f)
                took = count * 4 * 512 * wide / rate
                out[key] = (name + str(sign), took, 1.0, dep, 2 * unit + (key[3] != "f"))
                meta[key] = (name, h, far, sign, ox, oy, start * 4, count * 4)
                arrivals.append(key)

            delivered = {0: needs}
            for sign, at, piece in ring(f_n):
                key = (unit, part, sign, "f", 0, at)
                dep = needs if at == 0 else ((unit, part, sign, "f", 0, at - sign),)
                send(key, f_name, sign, at, 0, piece, dep)
                to = (at + sign) % f_n
                delivered[to] = delivered.get(to, ()) + (key,)
            for f in sorted(delivered, key=lambda v: min(v, f_n - v)):
                for sign, at, piece in ring(s_n, 1 if f % 2 == 0 else -1):
                    key = (unit, part, sign, "s", f, at)
                    dep = (
                        delivered[f] if at == 0 else ((unit, part, sign, "s", f, at - sign),)
                    )
                    send(key, s_name, sign, f, at, piece, dep)
        if unit == 0:
            early = arrivals
        for side in (far,) if far < 2 else (0, 1):
            for q in range(2):
                key = ("product", h, side, q)
                out[key] = ("tc", 0.8, 0.0, needs + tuple(arrivals) + splits, 0)
                products[h].append(key)
    for i, key in enumerate(splits):
        out[key] = ("tc", 0.5, 0.0, (early[4 + 6 * i],), 1)
    for h in range(2):
        out["core", h] = ("c", 0.7, 1.0, tuple(products[h]), 0)
        out["add", h] = ("tc", 0.3, 0.0, (("core", h),), 0)
        out["own", h] = ("tc", 0.2, 0.0, tuple(("sum", h, d) for d in range(1, Z)), 0)
        for d in (2, 1, 3):
            out["sum", h, d] = ("zz", 2.0, 1.5, (("add", h),), 0)
            out["spread", h, d] = ("zz", 2.0, 1.5, (("own", h),), 0)
        for d in range(Z):
            dep = ("spread", h, d) if d else ("own", h)
            out["share", h, d] = ("c", 0.2, 0.7, (dep,), 0)
    for key in out:
        if key not in meta and out[key][0] != "tc":
            meta[key] = key
    return out, meta


def gram_nodes():
    rate = 50e3
    out, meta, blocks = {}, {}, {}
    for part, (first, rows) in enumerate(((0, 16), (16, 8))):
        axes = (("y", Y), ("x", X)) if part == 0 else (("x", X), ("y", Y))
        (f_name, f_n), (s_name, s_n) = axes

        def send(key, name, sign, f, s, piece, dep):
            start, count = (first, rows) if piece is None else (first + 8 * piece, 8)
            ox, oy = (f, s) if f_name == "x" else (s, f)
            took = Z * count * 512 / rate
            out[key] = (name + str(sign), took, 1.0, dep, int(key[2] != "f"))
            meta[key] = (name, sign, ox, oy, start, count)
            to = (ox + sign) % X if name == "x" else ox % X
            blocks.setdefault(to, []).append(key)

        delivered = {0: ()}
        for sign, at, piece in ring(f_n, part):
            key = (part, sign, "f", 0, at)
            dep = () if at == 0 else ((part, sign, "f", 0, at - sign),)
            send(key, f_name, sign, at, 0, piece, dep)
            to = (at + sign) % f_n
            delivered[to] = delivered.get(to, ()) + (key,)
        for f in sorted(delivered, key=lambda v: min(v, f_n - v)):
            for sign, at, piece in ring(s_n, 1 if f % 2 == 0 else -1):
                key = (part, sign, "s", f, at)
                dep = delivered[f] if at == 0 else ((part, sign, "s", f, at - sign),)
                send(key, s_name, sign, f, at, piece, dep)
    for to, keys in blocks.items():
        out["core", to] = ("c", 1.0, 0.7, tuple(keys), 0)
        meta["core", to] = ("core", 0, to, 0, 0, Y * CHUNK)
    return out, meta


IMAGE_NODES, IMAGE_META = image_nodes()
IMAGE_EVENTS = order(IMAGE_NODES)
IMAGE_SLOT = {k: i for i, k in enumerate(IMAGE_META)}
GRAM_NODES, GRAM_META = gram_nodes()
GRAM_EVENTS = order(GRAM_NODES)
GRAM_SLOT = {k: i for i, k in enumerate(GRAM_META)}


def combine_kernel(
    factor_ref,
    panel_ref,
    image_ref,
    parts_ref,
    gathered,
    high,
    low,
    partial,
    from_core,
    from_z,
    local,
    from_y,
    total_x,
    from_x,
    from_line,
    p_send,
    p_recv,
    y_send,
    y_recv,
    x_send,
    x_recv,
    h_send,
    h_recv,
    g_send,
    g_recv,
):
    blk = lax.axis_index("blk")
    rd = lax.axis_index("rd")
    hi, x, y = blk // (X * Y), (blk // Y) % X, blk % Y
    z, core = rd // 2, rd % 2

    def at_blk(h, i, j):
        return (h * X + i) * Y + j

    def wrap(v, n):
        return lax.rem(v + n, n)

    def x_peer(d):
        return (at_blk(hi, wrap(x + d, X), y), rd)

    def y_peer(d):
        return (at_blk(hi, x, wrap(y + d, Y)), rd)

    def z_peer(d):
        return (blk, wrap(z + d, Z) * 2 + core)

    def line_peer(d, e):
        return (at_blk(1 - hi if e else hi, x, y), wrap(z + d, Z) * 2 + core)

    hi_peer = line_peer(0, 1)
    core_peer = (blk, z * 2 + 1 - core)

    def remote(src, dst, send, recv, peer):
        return pltpu.make_async_remote_copy(
            src_ref=src,
            dst_ref=dst,
            send_sem=send,
            recv_sem=recv,
            device_id=peer,
            device_id_type=MESH,
        )

    barrier = pltpu.get_barrier_semaphore()
    peers = [x_peer(d) for d in range(1, X)] + [y_peer(d) for d in range(1, Y)]
    peers += [line_peer(d, e) for e in range(2) for d in range(1 - e, Z)] + [core_peer]
    for peer in peers:
        pl.semaphore_signal(barrier, inc=1, device_id=peer, device_id_type=MESH)

    own = pl.ds(pl.multiple_of((x * Y + y) * HALF, 8), HALF)
    for h in range(2):
        gathered[h, hi, own, :] = panel_ref[h]
    pl.semaphore_wait(barrier, len(peers))

    my_rows = pl.ds(pl.multiple_of(core * (BLOCK // 2), 8), BLOCK // 2)
    other_rows = pl.ds(pl.multiple_of((1 - core) * (BLOCK // 2), 8), BLOCK // 2)

    def image_copy(key, arrived):
        kind, h, *more = IMAGE_META[key]
        if kind in ("x", "y", "hi"):
            far, sign, ox, oy, start, count = more
            if kind == "hi":
                peer = hi_peer
                side = 1 - hi if arrived else hi
            else:
                peer = x_peer(sign) if kind == "x" else y_peer(sign)
                side = (hi, 1 - hi, slice(None))[far]
                if arrived:
                    ox, oy = (ox + sign, oy) if kind == "x" else (ox, oy + sign)
            origin = wrap(x - ox % X, X) * Y + wrap(y - oy % Y, Y)
            rows = pl.ds(pl.multiple_of(origin * HALF + start, 8), count)
            src = dst = gathered.at[h, side, rows]
        elif kind == "core":
            peer = core_peer
            src, dst = partial.at[h, :, other_rows], from_core.at[h]
        elif kind == "sum":
            d = more[0]
            peer = z_peer(d)
            src, dst = from_core.at[h, wrap(z + d, Z)], from_z.at[h, d - 1]
        elif kind == "spread":
            d = more[0]
            peer = z_peer(d)
            src = dst = image_ref.at[4 * h + (wrap(z - d, Z) if arrived else z), my_rows]
        else:
            d = more[0]
            peer = core_peer
            rows = other_rows if arrived else my_rows
            src = dst = image_ref.at[4 * h + wrap(z - d, Z), rows]
        slot = IMAGE_SLOT[key]
        return remote(src, dst, p_send.at[slot], p_recv.at[slot], peer)

    def split(i):
        def some(n, carry):
            rows = pl.ds(pl.multiple_of(i * (BLOCK // SPLITS) + n * 16, 16), 16)
            high[rows, :], low[rows, :] = halves(factor_ref[rows, 0, :])
            return carry

        lax.fori_loop(0, BLOCK // SPLITS // 16, some, 0)

    def product(h, far, q):
        side = 1 - hi if far else hi
        right = jnp.concatenate(
            [gathered[h, side, pl.ds(2 * q + s, SIDE // 4, stride=4), :] for s in range(2)],
            axis=1,
        )
        top, rest = halves(right)
        span = pl.ds(pl.multiple_of(side * (SIDE // 4), 128), SIDE // 4)
        value = (
            jnp.dot(low[:, span], top, preferred_element_type=jnp.float32)
            + jnp.dot(high[:, span], rest, preferred_element_type=jnp.float32)
            + jnp.dot(high[:, span], top, preferred_element_type=jnp.float32)
        )
        for s in range(2):
            piece = value[:, s * 128 : s * 128 + 128]
            if far:
                piece = partial[h, 2 * q + s] + piece
            partial[h, 2 * q + s] = piece

    def add(h):
        for k in range(Z):
            from_core[h, k] += partial[h, k, my_rows, :]

    def own_sum(h):
        value = from_core[h, z] + from_z[h, 0] + from_z[h, 1] + from_z[h, 2]
        image_ref[4 * h + z, my_rows, :] = value

    tasks = dict(split=split, product=product, add=add, own=own_sum)
    for event, key in IMAGE_EVENTS:
        if event == "start":
            image_copy(key, False).start()
        elif event == "wait":
            image_copy(key, True).wait_recv()
        else:
            tasks[key[0]](*key[1:])
    for key in IMAGE_META:
        image_copy(key, False).wait_send()

    def group(g):
        return image_ref[g]

    mine = group(rd).T
    for d in range(4):
        local[d * 128 : d * 128 + 128, :] = jnp.dot(
            mine, group(wrap(rd + d, 8)), precision=HIGHEST, preferred_element_type=jnp.float32
        )
    lower_half = rd % 4
    local[512:640, :] = jnp.dot(
        group(lower_half).T,
        group(lower_half + 4),
        precision=HIGHEST,
        preferred_element_type=jnp.float32,
    )

    @pl.when(rd >= 4)
    def _():
        local[512:576, :] = local[576:640, :]

    for g in range(8):
        old = panel_ref[g // 4, pl.ds(g % 4, ROWS, stride=4), :]
        new = image_ref[g, pl.ds(rd * ROWS, ROWS), :]
        local[576 + g : 577 + g, :] = jnp.sum(old * new, axis=0, keepdims=True)
        local[584 + g : 585 + g, :] = jnp.sum(old * old, axis=0, keepdims=True)
    local[592:, :] = jnp.zeros((SLICE - 592, 128), jnp.float32)

    def to_x(d):
        rows = X_ROWS * wrap(x + d, X)
        where = pl.ds(pl.multiple_of(rows, 8), X_ROWS)
        return remote(
            local.at[where], from_x.at[d - 1], x_send.at[d - 1], x_recv.at[d - 1], x_peer(d)
        )

    for d in (2, 1, 3):
        to_x(d).start()
    for d in range(1, X):
        to_x(d).wait()
    strip = local[pl.ds(pl.multiple_of(x * X_ROWS, 8), X_ROWS), :]
    total_x[...] = (strip + from_x[0]) + (from_x[1] + from_x[2])

    def to_y(d):
        where = pl.ds(pl.multiple_of(wrap(y + d, Y) * CHUNK, 8), CHUNK)
        return remote(
            total_x.at[where], from_y.at[d - 1], y_send.at[d - 1], y_recv.at[d - 1], y_peer(d)
        )

    for d in (4, 3, 5, 2, 6, 1, 7):
        to_y(d).start()
    for d in range(1, Y):
        to_y(d).wait()
    chunk = total_x[pl.ds(pl.multiple_of(y * CHUNK, 8), CHUNK), :]
    for d in range(Y - 1):
        chunk = chunk + from_y[d]

    from_line[z, hi] = chunk

    def to_line(d, e, arrived):
        from_hi = 1 - hi if e and arrived else hi
        where = from_line.at[wrap(z - d, Z) if arrived else z, from_hi]
        slot = 2 * d + e
        return remote(where, where, h_send.at[slot], h_recv.at[slot], line_peer(d, e))

    line = [(d, e) for d in (2, 1, 3, 0) for e in (1, 0) if d or e]
    for d, e in line:
        to_line(d, e, False).start()
    here = pl.ds(pl.multiple_of((x * Y + y) * CHUNK, 8), CHUNK)
    for d, e in line:
        to_line(d, e, True).wait_recv()
    for d, e in line:
        to_line(d, e, False).wait_send()
    for k in range(Z):
        parts_ref[k, core, here, :] = (from_line[k, 0] + from_line[k, 1]) * (1.0 / N)

    def gram_copy(key, arrived):
        kind, sign, ox, oy, start, count = GRAM_META[key]
        slot = GRAM_SLOT[key]
        side, peer = core, core_peer
        if kind == "core":
            origin = wrap(x - ox, X) * Y
            side = 1 - core if arrived else core
        else:
            peer = x_peer(sign) if kind == "x" else y_peer(sign)
            if arrived:
                ox, oy = (ox + sign, oy) if kind == "x" else (ox, oy + sign)
            origin = wrap(x - ox % X, X) * Y + wrap(y - oy % Y, Y)
        rows = pl.ds(pl.multiple_of(origin * CHUNK + start, 8), count)
        where = parts_ref.at[:, side, rows]
        return remote(where, where, g_send.at[slot], g_recv.at[slot], peer)

    for event, key in GRAM_EVENTS:
        if event == "start":
            gram_copy(key, False).start()
        else:
            gram_copy(key, True).wait_recv()
    for key in GRAM_META:
        gram_copy(key, False).wait_send()


def combine(factor, panel):
    f32, bf16 = jnp.float32, jnp.bfloat16
    vmem = pl.BlockSpec(memory_space=pltpu.VMEM)

    def pair(n):
        return [pltpu.SemaphoreType.DMA((n,)), pltpu.SemaphoreType.DMA((n,))]

    return pl.pallas_call(
        combine_kernel,
        out_shape=(
            jax.ShapeDtypeStruct((8, BLOCK, 128), f32),
            jax.ShapeDtypeStruct((Z, 2, SLICE, 128), f32),
        ),
        in_specs=[vmem, vmem],
        out_specs=(vmem, vmem),
        scratch_shapes=[
            pltpu.VMEM((2, 2, SIDE, 128), f32),
            pltpu.VMEM((BLOCK, 8 * BLOCK), bf16),
            pltpu.VMEM((BLOCK, 8 * BLOCK), bf16),
            pltpu.VMEM((2, Z, BLOCK, 128), f32),
            pltpu.VMEM((2, Z, BLOCK // 2, 128), f32),
            pltpu.VMEM((2, Z - 1, BLOCK // 2, 128), f32),
            pltpu.VMEM((SLICE, 128), f32),
            pltpu.VMEM((Y - 1, CHUNK, 128), f32),
            pltpu.VMEM((X_ROWS, 128), f32),
            pltpu.VMEM((X - 1, X_ROWS, 128), f32),
            pltpu.VMEM((Z, 2, CHUNK, 128), f32),
            *pair(len(IMAGE_META)),
            *pair(Y - 1),
            *pair(X - 1),
            *pair(2 * Z),
            *pair(len(GRAM_META)),
        ],
        compiler_params=pltpu.CompilerParams(
            collective_id=0, has_side_effects=True, vmem_limit_bytes=50 << 20
        ),
        cost_estimate=pl.CostEstimate(
            flops=5 * 10**9, bytes_accessed=8 << 20, transcendentals=0
        ),
        name="combine",
    )(factor, panel)


def halves(value):
    top = value.astype(jnp.bfloat16)
    return top, (value - top.astype(jnp.float32)).astype(jnp.bfloat16)


def nt(a, b):
    def one(p, q):
        return lax.dot_general(
            p, q, (((1,), (1,)), ((), ())), preferred_element_type=jnp.float32
        )

    return one(a[1], b[0]) + one(a[0], b[1]) + one(a[0], b[0])


def invert_block(a, out_ref):
    sub = lax.broadcasted_iota(jnp.int32, (8, 128), 0)
    lane = lax.broadcasted_iota(jnp.int32, (8, 128), 1)
    left = [a[8 * g : 8 * g + 8, :] for g in range(16)]
    right = [jnp.where(lane == sub + 8 * g, 1.0, 0.0) for g in range(16)]

    def column(tile, at):
        return jnp.broadcast_to(tile[:, at : at + 1], (8, 128))

    def row(tile, at):
        return jnp.broadcast_to(tile[at : at + 1, :], (8, 128))

    for p in range(16):
        here, eye = left[p], right[p]
        cols = [column(here, 8 * p + k) for k in range(8)]
        heads, recips, pivots, marks = {}, [], [], []
        for k in range(8):
            d = row(cols[k], k)
            r = 1.0 / d
            m = jnp.where(sub > k, cols[k] * r, 0.0)
            u, w = row(here, k), row(eye, k)
            out_ref[8 * p + k : 8 * p + k + 1, :] = (w * lax.rsqrt(d))[0:1, :]
            for c in range(k + 1, 8):
                heads[k, c] = row(cols[c], k)
                cols[c] = cols[c] - m * heads[k, c]
            here = here - m * u
            eye = eye - m * w
            recips.append(r)
            pivots.append(u)
            marks.append(w)
        for g in range(p + 1, 16):
            tall = [column(left[g], 8 * p + k) for k in range(8)]
            lg, rg = left[g], right[g]
            for k in range(8):
                m = tall[k] * recips[k]
                for c in range(k + 1, 8):
                    tall[c] = tall[c] - m * heads[k, c]
                lg = lg - m * pivots[k]
                rg = rg - m * marks[k]
            left[g], right[g] = lg, rg


TALL = 1024 + BLOCK
PIECE = TALL // 4


def refresh_kernel(
    parts_ref, image_ref, panel_ref, values_ref, work, rest, high, low, inverse, w_high, w_low
):
    num = sq = None
    for r in range(8):
        at = r * SLICE + 576
        n_r, s_r = parts_ref[at : at + 8, :], parts_ref[at + 8 : at + 16, :]
        num = n_r if num is None else num + n_r
        sq = s_r if sq is None else sq + s_r
    values_ref[...] = num / (sq + 1e-06)
    for j in range(8):
        for i in range(j, 8):
            d, at, far = i - j, j * SLICE, i * SLICE
            if d == 4:
                block = jnp.concatenate(
                    [parts_ref[at + 512 : at + 576, :], parts_ref[far + 512 : far + 576, :]],
                    axis=0,
                ).T
            elif d < 4:
                block = parts_ref[at + d * 128 : at + d * 128 + 128, :]
                block = block.T if d else block
            else:
                block = parts_ref[far + (8 - d) * 128 : far + (8 - d) * 128 + 128, :]
            work[j, i * 128 : (i + 1) * 128, :] = block
        work[j, 1024:, :] = image_ref[j * BLOCK : (j + 1) * BLOCK, :]
    high[...] = jnp.zeros_like(high)
    low[...] = jnp.zeros_like(low)
    rest[...] = jnp.zeros_like(rest)
    inverse[...] = jnp.zeros_like(inverse)

    def step(j, carry):
        done = pl.ds(pl.multiple_of(jnp.maximum(j - 1, 0) * 128, 128), 128)
        rows = pl.ds(pl.multiple_of(j * 128, 128), 128)
        before = halves(inverse[...])
        w_high[...], w_low[...] = before
        strip = halves(nt(halves(rest[rows, :]), before))
        high[rows, done], low[rows, done] = strip
        side = (high[rows, :], low[rows, :])
        invert_block(work[j, rows, :] - nt(side, side), inverse)
        for n in range(4):
            span = slice(n * PIECE, (n + 1) * PIECE)
            solved = nt(halves(rest[span, :]), (w_high[...], w_low[...]))
            if n == 3:
                panel_ref[:, done] = solved[PIECE - BLOCK :, :]
            high[span, done], low[span, done] = halves(solved)
            rest[span, :] = work[j, span, :] - nt((high[span, :], low[span, :]), side)
        return carry

    lax.fori_loop(0, 8, step, 0)
    panel_ref[:, 896:] = nt(halves(rest[1024:, :]), halves(inverse[...]))


def refresh(parts, image):
    f32, bf16 = jnp.float32, jnp.bfloat16
    vmem = pl.BlockSpec(memory_space=pltpu.VMEM)
    return pl.pallas_call(
        refresh_kernel,
        out_shape=(
            jax.ShapeDtypeStruct((BLOCK, 1024), f32),
            jax.ShapeDtypeStruct((8, 128), f32),
        ),
        in_specs=[vmem, vmem],
        out_specs=(vmem, vmem),
        scratch_shapes=[
            pltpu.VMEM((8, TALL, 128), f32),
            pltpu.VMEM((TALL, 128), f32),
            pltpu.VMEM((TALL, 1024), bf16),
            pltpu.VMEM((TALL, 1024), bf16),
            pltpu.VMEM((128, 128), f32),
            pltpu.VMEM((128, 128), bf16),
            pltpu.VMEM((128, 128), bf16),
        ],
        compiler_params=pltpu.CompilerParams(vmem_limit_bytes=48 << 20),
        cost_estimate=pl.CostEstimate(
            flops=3 * 10**9, bytes_accessed=5 << 20, transcendentals=1024
        ),
        name="refresh",
    )(parts, image)


def body(factor, panel):
    image, parts = combine(
        factor, panel.reshape(ROWS, 2, 4, 128).transpose(1, 0, 2, 3).reshape(2, HALF, 128)
    )
    new_panel, values = refresh(
        parts.reshape(8 * SLICE, 128), image.reshape(8 * BLOCK, 128)
    )
    return (new_panel, values.reshape(1024))


def solution(mesh):
    placed = (P("blk", "rd", None), P(("blk", "rd"), None))
    return jax.shard_map(
        body, mesh=mesh, in_specs=placed, out_specs=(P("blk", None), P()), check_vma=False
    )
```

```python
import heapq

import jax
import jax.numpy as jnp
from jax import lax
from jax.experimental import pallas as pl
from jax.experimental.pallas import tpu as pltpu
from jax.sharding import PartitionSpec as P

N = 18432
X, Y, Z = 4, 8, 4
ROWS = 36
HALF = ROWS * 4
SIDE = X * Y * HALF
BLOCK = 288
CHUNK = 24
SLICE = X * Y * CHUNK
X_ROWS = Y * CHUNK
MESH = pl.DeviceIdType.MESH
HIGHEST = lax.Precision.HIGHEST


def ring(n, whole=0):
    h = n // 2
    for sign in (1, -1):
        for t in range(h - 1):
            yield sign, sign * t, None
        if whole == 0:
            yield sign, sign * (h - 1), 0 if sign > 0 else 1
        elif whole == sign:
            yield sign, sign * (h - 1), None


def order(nodes, ahead=2.0):
    waiting = {k: set(v[3]) for k, v in nodes.items()}
    followers = {}
    for k, v in nodes.items():
        for d in set(v[3]):
            followers.setdefault(d, []).append(k)
    free, queues, heap, events = {}, {}, [], []
    place = {k: i for i, k in enumerate(nodes)}

    def push(when, kind, what):
        push.count += 1
        heapq.heappush(heap, (when, push.count, kind, what))

    push.count = 0

    def pump(resource, now):
        queue = queues.setdefault(resource, [])
        reach = 0.0 if resource == "tc" else ahead
        while queue and free.get(resource, 0.0) - now <= reach:
            key = heapq.heappop(queue)[2]
            begin = max(now, free.get(resource, 0.0))
            free[resource] = begin + nodes[key][1]
            events.append(("task" if resource == "tc" else "start", key))
            push(free[resource] + nodes[key][2], "done", key)
        if queue:
            push(free[resource] - reach, "pump", resource)

    def ready(key, now):
        heapq.heappush(queues.setdefault(nodes[key][0], []), (nodes[key][4], place[key], key))
        pump(nodes[key][0], now)

    for k in nodes:
        if not waiting[k]:
            ready(k, 0.0)
    while heap:
        now, _, kind, what = heapq.heappop(heap)
        if kind == "pump":
            pump(what, now)
            continue
        if nodes[what][0] != "tc":
            events.append(("wait", what))
        for f in followers.get(what, ()):
            waiting[f].discard(what)
            if not waiting[f]:
                ready(f, now)
    assert not any(waiting.values())
    return events


SPLITS = 6


def image_nodes():
    rate = 50e3
    out, meta = {}, {}
    splits = tuple(("split", i) for i in range(SPLITS))
    products = {0: [], 1: []}
    early = []
    for unit, (h, far) in enumerate(((0, 0), (0, 1), (1, 0), (1, 1))):
        needs = ()
        if far:
            z_key = ("hi", h)
            before = (("hi", 0),) if h else ()
            out[z_key] = ("z", 6.0, 4.0, before, h)
            meta[z_key] = ("hi", h, 0, 0, 0, 0, 0, HALF)
            needs = (z_key,)
        arrivals = []
        for part, (first, rows) in enumerate(((0, 22), (22, 14))):
            axes = (("y", Y), ("x", X)) if part == 0 else (("x", X), ("y", Y))
            (f_name, f_n), (s_name, s_n) = axes
            big = (rows // 2 + 1) // 2 * 2

            def cut(piece):
                if piece is None:
                    return first, rows
                return (first, big) if piece == 0 else (first + big, rows - big)

            def send(key, name, sign, f, s, piece, dep):
                start, count = cut(piece)
                ox, oy = (f, s) if f_name == "x" else (s, f)
                took = count * 4 * 512 / rate
                out[key] = (name + str(sign), took, 1.0, dep, 2 * unit + (key[3] != "f"))
                meta[key] = (name, h, far, sign, ox, oy, start * 4, count * 4)
                arrivals.append(key)

            delivered = {0: needs}
            for sign, at, piece in ring(f_n):
                key = (unit, part, sign, "f", 0, at)
                dep = needs if at == 0 else ((unit, part, sign, "f", 0, at - sign),)
                send(key, f_name, sign, at, 0, piece, dep)
                to = (at + sign) % f_n
                delivered[to] = delivered.get(to, ()) + (key,)
            for f in sorted(delivered, key=lambda v: min(v, f_n - v)):
                for sign, at, piece in ring(s_n, 1 if f % 2 == 0 else -1):
                    key = (unit, part, sign, "s", f, at)
                    dep = (
                        delivered[f] if at == 0 else ((unit, part, sign, "s", f, at - sign),)
                    )
                    send(key, s_name, sign, f, at, piece, dep)
        if unit == 0:
            early = arrivals
        for q in range(2):
            key = ("product", h, far, q)
            last = (("product", h, 0, q),) if far else ()
            out[key] = ("tc", 0.8, 0.0, needs + tuple(arrivals) + splits + last, 0)
            products[h].append(key)
    for i, key in enumerate(splits):
        out[key] = ("tc", 0.5, 0.0, (early[4 + 6 * i],), 1)
    for h in range(2):
        out["core", h] = ("c", 0.7, 1.0, tuple(products[h]), 0)
        out["add", h] = ("tc", 0.3, 0.0, (("core", h),), 0)
        out["own", h] = ("tc", 0.2, 0.0, tuple(("sum", h, d) for d in range(1, Z)), 0)
        for d in (2, 1, 3):
            out["sum", h, d] = ("zz", 2.0, 1.5, (("add", h),), 0)
            out["spread", h, d] = ("zz", 2.0, 1.5, (("own", h),), 0)
        for d in range(Z):
            dep = ("spread", h, d) if d else ("own", h)
            out["share", h, d] = ("c", 0.2, 0.7, (dep,), 0)
    for key in out:
        if key not in meta and out[key][0] != "tc":
            meta[key] = key
    return out, meta


def gram_nodes():
    rate = 50e3
    out, meta, blocks = {}, {}, {}
    for part, (first, rows) in enumerate(((0, 16), (16, 8))):
        axes = (("y", Y), ("x", X)) if part == 0 else (("x", X), ("y", Y))
        (f_name, f_n), (s_name, s_n) = axes

        def send(key, name, sign, f, s, piece, dep):
            start, count = (first, rows) if piece is None else (first + 8 * piece, 8)
            ox, oy = (f, s) if f_name == "x" else (s, f)
            took = Z * count * 512 / rate
            out[key] = (name + str(sign), took, 1.0, dep, int(key[2] != "f"))
            meta[key] = (name, sign, ox, oy, start, count)
            to = (ox + sign) % X if name == "x" else ox % X
            blocks.setdefault(to, []).append(key)

        delivered = {0: ()}
        for sign, at, piece in ring(f_n, part):
            key = (part, sign, "f", 0, at)
            dep = () if at == 0 else ((part, sign, "f", 0, at - sign),)
            send(key, f_name, sign, at, 0, piece, dep)
            to = (at + sign) % f_n
            delivered[to] = delivered.get(to, ()) + (key,)
        for f in sorted(delivered, key=lambda v: min(v, f_n - v)):
            for sign, at, piece in ring(s_n, 1 if f % 2 == 0 else -1):
                key = (part, sign, "s", f, at)
                dep = delivered[f] if at == 0 else ((part, sign, "s", f, at - sign),)
                send(key, s_name, sign, f, at, piece, dep)
    for to, keys in blocks.items():
        out["core", to] = ("c", 1.0, 0.7, tuple(keys), 0)
        meta["core", to] = ("core", 0, to, 0, 0, Y * CHUNK)
    return out, meta


IMAGE_NODES, IMAGE_META = image_nodes()
IMAGE_EVENTS = order(IMAGE_NODES)
IMAGE_SLOT = {k: i for i, k in enumerate(IMAGE_META)}
GRAM_NODES, GRAM_META = gram_nodes()
GRAM_EVENTS = order(GRAM_NODES)
GRAM_SLOT = {k: i for i, k in enumerate(GRAM_META)}


def combine_kernel(
    factor_hbm,
    panel_ref,
    image_ref,
    parts_ref,
    factor_ref,
    factor_sem,
    gathered,
    high,
    low,
    partial,
    from_core,
    from_z,
    local,
    from_y,
    total_x,
    from_x,
    from_line,
    p_send,
    p_recv,
    y_send,
    y_recv,
    x_send,
    x_recv,
    h_send,
    h_recv,
    g_send,
    g_recv,
):
    blk = lax.axis_index("blk")
    rd = lax.axis_index("rd")
    hi, x, y = blk // (X * Y), (blk // Y) % X, blk % Y
    z, core = rd // 2, rd % 2

    def at_blk(h, i, j):
        return (h * X + i) * Y + j

    def wrap(v, n):
        return lax.rem(v + n, n)

    def x_peer(d):
        return (at_blk(hi, wrap(x + d, X), y), rd)

    def y_peer(d):
        return (at_blk(hi, x, wrap(y + d, Y)), rd)

    def z_peer(d):
        return (blk, wrap(z + d, Z) * 2 + core)

    def line_peer(d, e):
        return (at_blk(1 - hi if e else hi, x, y), wrap(z + d, Z) * 2 + core)

    hi_peer = line_peer(0, 1)
    core_peer = (blk, z * 2 + 1 - core)

    def remote(src, dst, send, recv, peer):
        return pltpu.make_async_remote_copy(
            src_ref=src,
            dst_ref=dst,
            send_sem=send,
            recv_sem=recv,
            device_id=peer,
            device_id_type=MESH,
        )

    load = pltpu.make_async_copy(factor_hbm, factor_ref, factor_sem)
    load.start()
    barrier = pltpu.get_barrier_semaphore()
    peers = [x_peer(d) for d in range(1, X)] + [y_peer(d) for d in range(1, Y)]
    peers += [line_peer(d, e) for e in range(2) for d in range(1 - e, Z)] + [core_peer]
    for peer in peers:
        pl.semaphore_signal(barrier, inc=1, device_id=peer, device_id_type=MESH)

    own = pl.ds(pl.multiple_of((x * Y + y) * HALF, 8), HALF)
    for h in range(2):
        gathered[h, hi, own, :] = panel_ref[h]
    pl.semaphore_wait(barrier, len(peers))

    my_rows = pl.ds(pl.multiple_of(core * (BLOCK // 2), 8), BLOCK // 2)
    other_rows = pl.ds(pl.multiple_of((1 - core) * (BLOCK // 2), 8), BLOCK // 2)

    def image_copy(key, arrived):
        kind, h, *more = IMAGE_META[key]
        if kind in ("x", "y", "hi"):
            far, sign, ox, oy, start, count = more
            if kind == "hi":
                peer = hi_peer
                side = 1 - hi if arrived else hi
            else:
                peer = x_peer(sign) if kind == "x" else y_peer(sign)
                side = 1 - hi if far else hi
                if arrived:
                    ox, oy = (ox + sign, oy) if kind == "x" else (ox, oy + sign)
            origin = wrap(x - ox % X, X) * Y + wrap(y - oy % Y, Y)
            rows = pl.ds(pl.multiple_of(origin * HALF + start, 8), count)
            src = dst = gathered.at[h, side, rows]
        elif kind == "core":
            peer = core_peer
            src, dst = partial.at[h, :, other_rows], from_core.at[h]
        elif kind == "sum":
            d = more[0]
            peer = z_peer(d)
            src, dst = from_core.at[h, wrap(z + d, Z)], from_z.at[h, d - 1]
        elif kind == "spread":
            d = more[0]
            peer = z_peer(d)
            src = dst = image_ref.at[4 * h + (wrap(z - d, Z) if arrived else z), my_rows]
        else:
            d = more[0]
            peer = core_peer
            rows = other_rows if arrived else my_rows
            src = dst = image_ref.at[4 * h + wrap(z - d, Z), rows]
        slot = IMAGE_SLOT[key]
        return remote(src, dst, p_send.at[slot], p_recv.at[slot], peer)

    def split(i):
        if i == 0:
            load.wait()

        def some(n, carry):
            rows = pl.ds(pl.multiple_of(i * (BLOCK // SPLITS) + n * 16, 16), 16)
            high[rows, :], low[rows, :] = halves(factor_ref[rows, 0, :])
            return carry

        lax.fori_loop(0, BLOCK // SPLITS // 16, some, 0)

    def product(h, far, q):
        side = 1 - hi if far else hi
        right = jnp.concatenate(
            [gathered[h, side, pl.ds(2 * q + s, SIDE // 4, stride=4), :] for s in range(2)],
            axis=1,
        )
        top, rest = halves(right)
        span = pl.ds(pl.multiple_of(side * (SIDE // 4), 128), SIDE // 4)
        value = (
            jnp.dot(low[:, span], top, preferred_element_type=jnp.float32)
            + jnp.dot(high[:, span], rest, preferred_element_type=jnp.float32)
            + jnp.dot(high[:, span], top, preferred_element_type=jnp.float32)
        )
        for s in range(2):
            piece = value[:, s * 128 : s * 128 + 128]
            if far:
                piece = partial[h, 2 * q + s] + piece
            partial[h, 2 * q + s] = piece

    def add(h):
        for k in range(Z):
            from_core[h, k] += partial[h, k, my_rows, :]

    def own_sum(h):
        value = from_core[h, z] + from_z[h, 0] + from_z[h, 1] + from_z[h, 2]
        image_ref[4 * h + z, my_rows, :] = value

    tasks = dict(split=split, product=product, add=add, own=own_sum)
    for event, key in IMAGE_EVENTS:
        if event == "start":
            image_copy(key, False).start()
        elif event == "wait":
            image_copy(key, True).wait_recv()
        else:
            tasks[key[0]](*key[1:])
    for key in IMAGE_META:
        image_copy(key, False).wait_send()

    def group(g):
        return image_ref[g]

    mine = group(rd).T
    for d in range(4):
        local[d * 128 : d * 128 + 128, :] = jnp.dot(
            mine, group(wrap(rd + d, 8)), precision=HIGHEST, preferred_element_type=jnp.float32
        )
    lower_half = rd % 4
    local[512:640, :] = jnp.dot(
        group(lower_half).T,
        group(lower_half + 4),
        precision=HIGHEST,
        preferred_element_type=jnp.float32,
    )

    @pl.when(rd >= 4)
    def _():
        local[512:576, :] = local[576:640, :]

    for g in range(8):
        old = panel_ref[g // 4, pl.ds(g % 4, ROWS, stride=4), :]
        new = image_ref[g, pl.ds(rd * ROWS, ROWS), :]
        local[576 + g : 577 + g, :] = jnp.sum(old * new, axis=0, keepdims=True)
        local[584 + g : 585 + g, :] = jnp.sum(old * old, axis=0, keepdims=True)
    local[592:, :] = jnp.zeros((SLICE - 592, 128), jnp.float32)

    def to_x(d):
        rows = X_ROWS * wrap(x + d, X)
        where = pl.ds(pl.multiple_of(rows, 8), X_ROWS)
        return remote(
            local.at[where], from_x.at[d - 1], x_send.at[d - 1], x_recv.at[d - 1], x_peer(d)
        )

    for d in (2, 1, 3):
        to_x(d).start()
    for d in range(1, X):
        to_x(d).wait()
    strip = local[pl.ds(pl.multiple_of(x * X_ROWS, 8), X_ROWS), :]
    total_x[...] = (strip + from_x[0]) + (from_x[1] + from_x[2])

    def to_y(d):
        where = pl.ds(pl.multiple_of(wrap(y + d, Y) * CHUNK, 8), CHUNK)
        return remote(
            total_x.at[where], from_y.at[d - 1], y_send.at[d - 1], y_recv.at[d - 1], y_peer(d)
        )

    for d in (4, 3, 5, 2, 6, 1, 7):
        to_y(d).start()
    for d in range(1, Y):
        to_y(d).wait()
    chunk = total_x[pl.ds(pl.multiple_of(y * CHUNK, 8), CHUNK), :]
    for d in range(Y - 1):
        chunk = chunk + from_y[d]

    from_line[z, hi] = chunk

    def to_line(d, e, arrived):
        from_hi = 1 - hi if e and arrived else hi
        where = from_line.at[wrap(z - d, Z) if arrived else z, from_hi]
        slot = 2 * d + e
        return remote(where, where, h_send.at[slot], h_recv.at[slot], line_peer(d, e))

    line = [(d, e) for d in (2, 1, 3, 0) for e in (1, 0) if d or e]
    for d, e in line:
        to_line(d, e, False).start()
    here = pl.ds(pl.multiple_of((x * Y + y) * CHUNK, 8), CHUNK)
    for d, e in line:
        to_line(d, e, True).wait_recv()
    for d, e in line:
        to_line(d, e, False).wait_send()
    for k in range(Z):
        parts_ref[k, core, here, :] = (from_line[k, 0] + from_line[k, 1]) * (1.0 / N)

    def gram_copy(key, arrived):
        kind, sign, ox, oy, start, count = GRAM_META[key]
        slot = GRAM_SLOT[key]
        side, peer = core, core_peer
        if kind == "core":
            origin = wrap(x - ox, X) * Y
            side = 1 - core if arrived else core
        else:
            peer = x_peer(sign) if kind == "x" else y_peer(sign)
            if arrived:
                ox, oy = (ox + sign, oy) if kind == "x" else (ox, oy + sign)
            origin = wrap(x - ox % X, X) * Y + wrap(y - oy % Y, Y)
        rows = pl.ds(pl.multiple_of(origin * CHUNK + start, 8), count)
        where = parts_ref.at[:, side, rows]
        return remote(where, where, g_send.at[slot], g_recv.at[slot], peer)

    for event, key in GRAM_EVENTS:
        if event == "start":
            gram_copy(key, False).start()
        else:
            gram_copy(key, True).wait_recv()
    for key in GRAM_META:
        gram_copy(key, False).wait_send()


def combine(factor, panel):
    f32, bf16 = jnp.float32, jnp.bfloat16
    vmem = pl.BlockSpec(memory_space=pltpu.VMEM)

    def pair(n):
        return [pltpu.SemaphoreType.DMA((n,)), pltpu.SemaphoreType.DMA((n,))]

    return pl.pallas_call(
        combine_kernel,
        out_shape=(
            jax.ShapeDtypeStruct((8, BLOCK, 128), f32),
            jax.ShapeDtypeStruct((Z, 2, SLICE, 128), f32),
        ),
        in_specs=[pl.BlockSpec(memory_space=pl.ANY), vmem],
        out_specs=(vmem, vmem),
        scratch_shapes=[
            pltpu.VMEM((BLOCK, 1, 8 * BLOCK), f32),
            pltpu.SemaphoreType.DMA(()),
            pltpu.VMEM((2, 2, SIDE, 128), f32),
            pltpu.VMEM((BLOCK, 8 * BLOCK), bf16),
            pltpu.VMEM((BLOCK, 8 * BLOCK), bf16),
            pltpu.VMEM((2, Z, BLOCK, 128), f32),
            pltpu.VMEM((2, Z, BLOCK // 2, 128), f32),
            pltpu.VMEM((2, Z - 1, BLOCK // 2, 128), f32),
            pltpu.VMEM((SLICE, 128), f32),
            pltpu.VMEM((Y - 1, CHUNK, 128), f32),
            pltpu.VMEM((X_ROWS, 128), f32),
            pltpu.VMEM((X - 1, X_ROWS, 128), f32),
            pltpu.VMEM((Z, 2, CHUNK, 128), f32),
            *pair(len(IMAGE_META)),
            *pair(Y - 1),
            *pair(X - 1),
            *pair(2 * Z),
            *pair(len(GRAM_META)),
        ],
        compiler_params=pltpu.CompilerParams(
            collective_id=0, has_side_effects=True, vmem_limit_bytes=58 << 20
        ),
        cost_estimate=pl.CostEstimate(
            flops=5 * 10**9, bytes_accessed=8 << 20, transcendentals=0
        ),
        name="combine",
    )(factor, panel)


def halves(value):
    top = value.astype(jnp.bfloat16)
    return top, (value - top.astype(jnp.float32)).astype(jnp.bfloat16)


def nt(a, b):
    def one(p, q):
        return lax.dot_general(
            p, q, (((1,), (1,)), ((), ())), preferred_element_type=jnp.float32
        )

    return one(a[1], b[0]) + one(a[0], b[1]) + one(a[0], b[0])


def invert_block(a, out_ref):
    sub = lax.broadcasted_iota(jnp.int32, (8, 128), 0)
    lane = lax.broadcasted_iota(jnp.int32, (8, 128), 1)
    left = [a[8 * g : 8 * g + 8, :] for g in range(16)]
    right = [jnp.where(lane == sub + 8 * g, 1.0, 0.0) for g in range(16)]

    def column(tile, at):
        return jnp.broadcast_to(tile[:, at : at + 1], (8, 128))

    def row(tile, at):
        return jnp.broadcast_to(tile[at : at + 1, :], (8, 128))

    for p in range(16):
        here, eye = left[p], right[p]
        cols = [column(here, 8 * p + k) for k in range(8)]
        heads, recips, pivots, marks = {}, [], [], []
        for k in range(8):
            d = row(cols[k], k)
            r = 1.0 / d
            m = jnp.where(sub > k, cols[k] * r, 0.0)
            u, w = row(here, k), row(eye, k)
            out_ref[8 * p + k : 8 * p + k + 1, :] = (w * lax.rsqrt(d))[0:1, :]
            for c in range(k + 1, 8):
                heads[k, c] = row(cols[c], k)
                cols[c] = cols[c] - m * heads[k, c]
            here = here - m * u
            eye = eye - m * w
            recips.append(r)
            pivots.append(u)
            marks.append(w)
        for g in range(p + 1, 16):
            tall = [column(left[g], 8 * p + k) for k in range(8)]
            lg, rg = left[g], right[g]
            for k in range(8):
                m = tall[k] * recips[k]
                for c in range(k + 1, 8):
                    tall[c] = tall[c] - m * heads[k, c]
                lg = lg - m * pivots[k]
                rg = rg - m * marks[k]
            left[g], right[g] = lg, rg


TALL = 1024 + BLOCK
PIECE = TALL // 4


def refresh_kernel(
    parts_ref, image_ref, panel_ref, values_ref, work, rest, high, low, inverse, w_high, w_low
):
    num = sq = None
    for r in range(8):
        at = r * SLICE + 576
        n_r, s_r = parts_ref[at : at + 8, :], parts_ref[at + 8 : at + 16, :]
        num = n_r if num is None else num + n_r
        sq = s_r if sq is None else sq + s_r
    values_ref[...] = num / (sq + 1e-06)
    for j in range(8):
        for i in range(j, 8):
            d, at, far = i - j, j * SLICE, i * SLICE
            if d == 4:
                block = jnp.concatenate(
                    [parts_ref[at + 512 : at + 576, :], parts_ref[far + 512 : far + 576, :]],
                    axis=0,
                ).T
            elif d < 4:
                block = parts_ref[at + d * 128 : at + d * 128 + 128, :]
                block = block.T if d else block
            else:
                block = parts_ref[far + (8 - d) * 128 : far + (8 - d) * 128 + 128, :]
            work[j, i * 128 : (i + 1) * 128, :] = block
        work[j, 1024:, :] = image_ref[j * BLOCK : (j + 1) * BLOCK, :]
    high[...] = jnp.zeros_like(high)
    low[...] = jnp.zeros_like(low)
    rest[...] = jnp.zeros_like(rest)
    inverse[...] = jnp.zeros_like(inverse)

    def step(j, carry):
        done = pl.ds(pl.multiple_of(jnp.maximum(j - 1, 0) * 128, 128), 128)
        rows = pl.ds(pl.multiple_of(j * 128, 128), 128)
        before = halves(inverse[...])
        w_high[...], w_low[...] = before
        strip = halves(nt(halves(rest[rows, :]), before))
        high[rows, done], low[rows, done] = strip
        side = (high[rows, :], low[rows, :])
        invert_block(work[j, rows, :] - nt(side, side), inverse)
        for n in range(4):
            span = slice(n * PIECE, (n + 1) * PIECE)
            solved = nt(halves(rest[span, :]), (w_high[...], w_low[...]))
            if n == 3:
                panel_ref[:, done] = solved[PIECE - BLOCK :, :]
            high[span, done], low[span, done] = halves(solved)
            rest[span, :] = work[j, span, :] - nt((high[span, :], low[span, :]), side)
        return carry

    lax.fori_loop(0, 8, step, 0)
    panel_ref[:, 896:] = nt(halves(rest[1024:, :]), halves(inverse[...]))


def refresh(parts, image):
    f32, bf16 = jnp.float32, jnp.bfloat16
    vmem = pl.BlockSpec(memory_space=pltpu.VMEM)
    return pl.pallas_call(
        refresh_kernel,
        out_shape=(
            jax.ShapeDtypeStruct((BLOCK, 1024), f32),
            jax.ShapeDtypeStruct((8, 128), f32),
        ),
        in_specs=[vmem, vmem],
        out_specs=(vmem, vmem),
        scratch_shapes=[
            pltpu.VMEM((8, TALL, 128), f32),
            pltpu.VMEM((TALL, 128), f32),
            pltpu.VMEM((TALL, 1024), bf16),
            pltpu.VMEM((TALL, 1024), bf16),
            pltpu.VMEM((128, 128), f32),
            pltpu.VMEM((128, 128), bf16),
            pltpu.VMEM((128, 128), bf16),
        ],
        compiler_params=pltpu.CompilerParams(vmem_limit_bytes=48 << 20),
        cost_estimate=pl.CostEstimate(
            flops=3 * 10**9, bytes_accessed=5 << 20, transcendentals=1024
        ),
        name="refresh",
    )(parts, image)


def body(factor, panel):
    image, parts = combine(
        factor, panel.reshape(ROWS, 2, 4, 128).transpose(1, 0, 2, 3).reshape(2, HALF, 128)
    )
    new_panel, values = refresh(
        parts.reshape(8 * SLICE, 128), image.reshape(8 * BLOCK, 128)
    )
    return (new_panel, values.reshape(1024))


def solution(mesh):
    placed = (P("blk", "rd", None), P(("blk", "rd"), None))
    return jax.shard_map(
        body, mesh=mesh, in_specs=placed, out_specs=(P("blk", None), P()), check_vma=False
    )
```
